32 devices in a mesh: uly: 8 (over y, x, core), blk: 4 (over z).
Axes of the slice: x: 2, y: 2, z: 4, core: 2. Of those that a mesh axis runs over, the one named last changes fastest.
Arguments:
- queries: bfloat16 [4096, 32, 128], P(('blk', 'uly')), may hold values from -6 to 6
- keys: bfloat16 [4096, 8, 128], P(('blk', 'uly')), may hold values from -6 to 6
- values: bfloat16 [4096, 8, 128], P(('blk', 'uly')), may hold values from -6 to 6
- grad_out: bfloat16 [4096, 32, 128], P(('blk', 'uly')), may hold values from -6 to 6
- lse: float32 [32, 4096], P('uly'), may hold values from 4 to 6
- delta: float32 [32, 4096], P('uly'), may hold values from -18 to 18
- block_keys: int32 [32, 5], replicated, may hold values from -1 to 31, as said below
Outputs:
- grad_queries: bfloat16 [4096, 32, 128], P(('blk', 'uly'))
- grad_keys: bfloat16 [4096, 8, 128], P(('blk', 'uly'))
- grad_values: bfloat16 [4096, 8, 128], P(('blk', 'uly'))
The draws below stay inside these ranges and needn't reach their ends.
Inputs may be any that keep to these rules, and one draw needn't show every extreme that they name: `block_keys`: query block b lists itself first, then 5 - 1 distinct earlier blocks c with c >= 8 * (b // 8 - 1); entries are -1 only where fewer earlier blocks exist, after the listed ones.
All inputs are finite; a program needn't handle non-finite values.
Results may differ from the reference program's by a relative error of at most 0.0053.
Values may be sent and summed in bfloat16 or wider, within the bound.
No kernel may reach another device: no remote copies, remote signals or barrier semaphores. Data moves between devices by JAX's collectives and lax.ppermute only.
A program may use at most 128 MiB of HBM per device.

```python
import math
import jax
import jax.numpy as jnp
from jax import lax

HEADS = 32
KVH = 8
HD = 128
BLOCK = 128
KSEL = 5
SLAB_BLOCKS = 8
SEQ = 4096
NBLOCKS = 32


def draw_block_keys(key, part):
    block_ids = jnp.arange(NBLOCKS, dtype=jnp.int32)
    span = 2 * SLAB_BLOCKS - 1
    offsets = jnp.arange(span, dtype=jnp.int32)
    lowest = jnp.maximum(0, (block_ids // SLAB_BLOCKS - 1) * SLAB_BLOCKS)
    candidate = block_ids[:, None] - 1 - offsets[None, :]
    usable = candidate >= lowest[:, None]
    raw_scores = jax.random.randint(key, (NBLOCKS, span), 0, 1 << 20, dtype=jnp.int32)
    ranked = jnp.where(usable, raw_scores * (2 * SLAB_BLOCKS) + offsets[None, :], -1)
    best, where_best = lax.top_k(ranked, KSEL - 1)
    picked = jnp.where(best >= 0, block_ids[:, None] - 1 - where_best.astype(jnp.int32), -1)
    return jnp.concatenate([block_ids[:, None], picked], axis=1).astype(jnp.int32)


def block_levels(rng, dims, shards, least, high):
    loudness = 1.0
    for dim, shards_of in shards:
        heights = jax.random.uniform(jax.random.fold_in(jax.random.fold_in(rng, 6), dim), (shards_of,), jnp.float32, least / len(shards), high / len(shards))
        loudness = loudness * jnp.repeat(jnp.exp(heights), dims[dim] // shards_of).reshape((-1,) + (1,) * (len(dims) - 1 - dim))
    return loudness


def scatter_about(stream_key, dims, scale, reach, cuts=(), held_as=jnp.bfloat16):
    drawn = scale * jax.random.normal(stream_key, dims, jnp.float32)
    if cuts:
        drawn = drawn * block_levels(stream_key, dims, cuts, -0.22, 0.18)
    return jnp.clip(drawn, -reach, reach).astype(held_as)


def setup_inputs(seed: int = 0) -> dict:
    splits = jax.random.split(jax.random.key(seed), 8)
    return {
        "queries": scatter_about(splits[0], (SEQ, HEADS, HD), 1.0, 6.0, ((0, 32),)),
        "keys": scatter_about(splits[1], (SEQ, KVH, HD), 1.0, 6.0, ((0, 32),)),
        "values": scatter_about(splits[2], (SEQ, KVH, HD), 1.0, 6.0, ((0, 32),)),
        "grad_out": scatter_about(splits[3], (SEQ, HEADS, HD), 1.0, 6.0, ((0, 32),)),
        "lse": jnp.clip(4.0 + 2.0 * jax.random.uniform(splits[4], (HEADS, SEQ), jnp.float32) ** block_levels(splits[4], (HEADS, SEQ), ((0, 8),), -0.2, 0.2), 4.0, 6.0),
        "delta": scatter_about(splits[5], (HEADS, SEQ), 3.0, 18.0, ((0, 8),), jnp.float32),
        "block_keys": draw_block_keys(jax.random.fold_in(splits[7], 71), 0),
    }


def block_grads(query_rows, dout_rows, lse_rows, delta_rows, key_blocks, value_blocks, block_index, block_valid, block_diag, per_step):
    query_blocks = block_index.shape[0]
    width = key_blocks.shape[1]
    head_dim = key_blocks.shape[2]
    head_count = query_rows.shape[1]
    select = block_index.shape[1]
    step_count = query_blocks // per_step
    score_scale = 1.0 / math.sqrt(head_dim)
    query_steps = query_rows.reshape(step_count, per_step, width, head_count, head_dim)
    dout_steps = dout_rows.reshape(step_count, per_step, width, head_count, head_dim)
    lse_steps = lse_rows.reshape(head_count, step_count, per_step, width).transpose(1, 2, 0, 3)
    delta_steps = delta_rows.reshape(head_count, step_count, per_step, width).transpose(1, 2, 0, 3)
    safe_index = jnp.where(block_valid, block_index, 0).astype(jnp.int32).reshape(step_count, per_step, select)
    valid_steps = block_valid.reshape(step_count, per_step, select)
    diag_steps = block_diag.reshape(step_count, per_step, select)
    positions = jnp.arange(width, dtype=jnp.int32)
    causal = positions[None, :] <= positions[:, None]

    def advance(carry, inputs):
        key_acc, value_acc = carry
        query_part, dout_part, lse_part, delta_part, index_part, valid_part, diag_part = inputs
        key_part = key_blocks[index_part].astype(jnp.float32)
        value_part = value_blocks[index_part].astype(jnp.float32)
        query_wide = query_part.astype(jnp.float32)
        dout_wide = dout_part.astype(jnp.float32)
        scores = jnp.einsum('pthd,pjsd->phtjs', query_wide, key_part) * score_scale
        allowed = valid_part[:, None, None, :, None] & (jnp.logical_not(diag_part)[:, None, None, :, None] | causal[None, None, :, None, :])
        probs = jnp.where(allowed, jnp.exp(scores - lse_part[:, :, :, None, None]), 0.0)
        dprobs = jnp.einsum('pthd,pjsd->phtjs', dout_wide, value_part)
        dscores = probs * (dprobs - delta_part[:, :, :, None, None])
        probs_low = probs.astype(jnp.bfloat16).astype(jnp.float32)
        dscores_low = dscores.astype(jnp.bfloat16).astype(jnp.float32)
        grad_query = jnp.einsum('phtjs,pjsd->pthd', dscores_low, key_part) * score_scale
        grad_value = jnp.einsum('phtjs,pthd->pjsd', probs_low, dout_wide)
        grad_key = jnp.einsum('phtjs,pthd->pjsd', dscores_low, query_wide) * score_scale
        flat_index = index_part.reshape(-1)
        key_acc = key_acc.at[flat_index].add(grad_key.reshape(-1, width, head_dim))
        value_acc = value_acc.at[flat_index].add(grad_value.reshape(-1, width, head_dim))
        return ((key_acc, value_acc), grad_query)
    start = jnp.zeros((key_blocks.shape[0], width, head_dim), jnp.float32)
    (key_acc, value_acc), grad_query = lax.scan(advance, (start, start), (query_steps, dout_steps, lse_steps, delta_steps, safe_index, valid_steps, diag_steps))
    return (grad_query.reshape(query_blocks * width, head_count, head_dim), key_acc, value_acc)

def reference(queries, keys, values, grad_out, lse, delta, block_keys):
    seq_len = queries.shape[0]
    block_total = seq_len // BLOCK
    group = HEADS // KVH
    per_step = math.gcd(block_total, max(1, 512 // BLOCK))
    block_ids = jnp.arange(block_total, dtype=jnp.int32)
    block_valid = block_keys >= 0
    block_diag = block_keys == block_ids[:, None]

    def one_group(kv_index):
        query_rows = lax.dynamic_slice_in_dim(queries, kv_index * group, group, 1)
        dout_rows = lax.dynamic_slice_in_dim(grad_out, kv_index * group, group, 1)
        lse_rows = lax.dynamic_slice_in_dim(lse, kv_index * group, group, 0)
        delta_rows = lax.dynamic_slice_in_dim(delta, kv_index * group, group, 0)
        key_blocks = lax.dynamic_slice_in_dim(keys, kv_index, 1, 1).reshape(block_total, BLOCK, HD)
        value_blocks = lax.dynamic_slice_in_dim(values, kv_index, 1, 1).reshape(block_total, BLOCK, HD)
        return block_grads(query_rows, dout_rows, lse_rows, delta_rows, key_blocks, value_blocks, block_keys, block_valid, block_diag, per_step)
    grad_query, grad_key, grad_value = lax.map(one_group, jnp.arange(KVH, dtype=jnp.int32))
    grad_queries = grad_query.transpose(1, 0, 2, 3).reshape(seq_len, HEADS, HD).astype(jnp.bfloat16)
    grad_keys = grad_key.reshape(KVH, seq_len, HD).transpose(1, 0, 2).astype(jnp.bfloat16)
    grad_values = grad_value.reshape(KVH, seq_len, HD).transpose(1, 0, 2).astype(jnp.bfloat16)
    return (grad_queries, grad_keys, grad_values)
```

```python
import functools
import math

import jax
import jax.numpy as jnp
from jax import lax
from jax.experimental import pallas as pl
from jax.experimental.pallas import tpu as pltpu
from jax.sharding import PartitionSpec as P

BLOCK = 128
LOG2E = 1.4426950408889634


def contract(a, b, a_dim, b_dim):
    return lax.dot_general(a, b, (((a_dim,), (b_dim,)), ((), ())), preferred_element_type=jnp.float32)


def block_kernel(slab_ref, keys_ref, qd_ref, own_ref, prev_ref, lse_ref, delta_ref, dq_ref, own_out, prev_out, kv, kt, acc, cat_k, cat_v, cat_t):
    slab_blocks = qd_ref.shape[0]
    heads = qd_ref.shape[2]
    select = keys_ref.shape[1]
    rows = heads * BLOCK
    head_dim = qd_ref.shape[4]
    scale = 1.0 / math.sqrt(head_dim)
    first = slab_ref[0] * slab_blocks

    def stage(c, _):
        for half, ref in ((0, prev_ref), (1, own_ref)):
            at = half * slab_blocks + c
            kv[0, at] = ref[c, 0]
            kv[1, at] = ref[c, 1]
            kt[at] = ref[c, 0].T
        return _

    lax.fori_loop(0, slab_blocks, stage, 0)
    acc[...] = jnp.zeros_like(acc)
    key_pos = lax.broadcasted_iota(jnp.int32, (BLOCK, rows), 0)
    query_pos = lax.broadcasted_iota(jnp.int32, (BLOCK, rows), 1) % BLOCK
    causal = key_pos <= query_pos

    def query_block(b, _):
        q = qd_ref[b, 0].reshape(rows, head_dim)
        do = qd_ref[b, 1].reshape(rows, head_dim)
        entries = [keys_ref[first + b, j] for j in range(select)]
        places = [jnp.where(e >= 0, e - first + slab_blocks, 0) for e in entries]
        for j in range(select):
            cat_k[pl.ds(j * BLOCK, BLOCK)] = kv[0, places[j]]
            cat_v[pl.ds(j * BLOCK, BLOCK)] = kv[1, places[j]]
            cat_t[:, pl.ds(j * BLOCK, BLOCK)] = kt[places[j]]
        lanes = pl.ds(pl.multiple_of((first + b) * BLOCK, BLOCK), BLOCK)
        lse = jnp.concatenate([lse_ref[pl.ds(h, 1), lanes] for h in range(heads)], 1) * LOG2E
        delta = jnp.concatenate([delta_ref[pl.ds(h, 1), lanes] for h in range(heads)], 1)
        s = contract(cat_k[...], q, 1, 1)
        dp = contract(cat_v[...], do, 1, 1)
        p_parts = []
        for j in range(select):
            p = jnp.exp2(s[j * BLOCK : (j + 1) * BLOCK] * (scale * LOG2E) - lse)
            allowed = causal if j == 0 else entries[j] >= 0
            p_parts.append(jnp.where(allowed, p, 0.0))
        p = jnp.concatenate(p_parts, 0)
        ds = (p * (dp - delta)).astype(jnp.bfloat16)
        dv = contract(p.astype(jnp.bfloat16), do, 1, 0)
        dk = contract(ds, q, 1, 0)
        dqt = contract(cat_t[...], ds, 1, 0) * scale
        dq_ref[b] = dqt.T.astype(jnp.bfloat16).reshape(heads, BLOCK, head_dim)
        for j in range(select):
            part = slice(j * BLOCK, (j + 1) * BLOCK)
            acc[0, places[j]] += dk[part]
            acc[1, places[j]] += dv[part]
        return _

    lax.fori_loop(0, slab_blocks, query_block, 0)

    def finish(c, _):
        prev_out[c, 0] = (acc[0, c] * scale).astype(prev_out.dtype)
        prev_out[c, 1] = acc[1, c].astype(prev_out.dtype)
        own_out[c, 0] = acc[0, slab_blocks + c] * scale
        own_out[c, 1] = acc[1, slab_blocks + c]
        return _

    lax.fori_loop(0, slab_blocks, finish, 0)


def block_grads(slab, block_keys, qd, own, prev, lse, delta):
    slab_blocks, _, heads, _, head_dim = qd.shape
    select = block_keys.shape[1]
    smem = pl.BlockSpec(memory_space=pltpu.SMEM)
    vmem = pl.BlockSpec(memory_space=pltpu.VMEM)
    kv_shape = (slab_blocks, 2, BLOCK, head_dim)
    wide = select * BLOCK
    macs = slab_blocks * heads * select * 5 * BLOCK * BLOCK * head_dim
    return pl.pallas_call(
        block_kernel,
        in_specs=[smem, smem, vmem, vmem, vmem, vmem, vmem],
        out_specs=[vmem, vmem, vmem],
        out_shape=[
            jax.ShapeDtypeStruct((slab_blocks, heads, BLOCK, head_dim), jnp.bfloat16),
            jax.ShapeDtypeStruct(kv_shape, jnp.float32),
            jax.ShapeDtypeStruct(kv_shape, jnp.bfloat16),
        ],
        scratch_shapes=[
            pltpu.VMEM((2, 2 * slab_blocks, BLOCK, head_dim), jnp.bfloat16),
            pltpu.VMEM((2 * slab_blocks, head_dim, BLOCK), jnp.bfloat16),
            pltpu.VMEM((2, 2 * slab_blocks, BLOCK, head_dim), jnp.float32),
            pltpu.VMEM((wide, head_dim), jnp.bfloat16),
            pltpu.VMEM((wide, head_dim), jnp.bfloat16),
            pltpu.VMEM((head_dim, wide), jnp.bfloat16),
        ],
        compiler_params=pltpu.CompilerParams(vmem_limit_bytes=48 * 1024 * 1024),
        cost_estimate=pl.CostEstimate(flops=2 * macs, bytes_accessed=8 * 1024 * 1024, transcendentals=0),
    )(slab, block_keys, qd, own, prev, lse, delta)


def passed_along(block, axis, distance):
    devices = range(lax.axis_size(axis))
    return lax.ppermute(block, axis, [(i - distance, i) for i in devices if i - distance in devices])


def exchange(x):
    return lax.all_to_all(x, "uly", split_axis=0, concat_axis=0, tiled=True)


def by_head(x, uly_count):
    tokens, heads, head_dim = x.shape
    return x.reshape(tokens, uly_count, heads // uly_count, head_dim).transpose(1, 2, 0, 3)


def shards(queries, keys, values, grad_out, lse, delta, block_keys):
    uly_count = lax.axis_size("uly")
    tokens_here, head_total, head_dim = queries.shape
    kv_heads = keys.shape[1]
    fold_count = uly_count // kv_heads
    heads = head_total // uly_count
    slab = lax.axis_index("blk").reshape(1)

    kv = jnp.stack([keys.transpose(1, 0, 2), values.transpose(1, 0, 2)], 1)
    own = exchange(jnp.repeat(kv, fold_count, axis=0))
    prev = passed_along(own, "blk", 1)
    qd = exchange(jnp.stack([by_head(queries, uly_count), by_head(grad_out, uly_count)], 1))
    dq, own_grad, prev_grad = block_grads(slab, block_keys, qd, own, prev, lse, delta)
    back = passed_along(prev_grad, "blk", -1)
    grad_queries = exchange(dq)
    grad_queries = grad_queries.reshape(head_total, tokens_here, head_dim).transpose(1, 0, 2)
    kv_grad = exchange((own_grad + back.astype(jnp.float32)).astype(jnp.bfloat16))
    kv_grad = kv_grad.reshape(kv_heads, fold_count, 2, tokens_here, head_dim).astype(jnp.float32).sum(1)
    kv_grad = kv_grad.transpose(1, 2, 0, 3).astype(jnp.bfloat16)
    return grad_queries, kv_grad[0], kv_grad[1]


def solution(mesh):
    spread = P(("blk", "uly"), None, None)
    return jax.shard_map(
        shards,
        mesh=mesh,
        in_specs=(spread, spread, spread, spread, P("uly", None), P("uly", None), P()),
        out_specs=(spread, spread, spread),
        check_vma=False,
    )
```

```python
import functools
import math

import jax
import jax.numpy as jnp
from jax import lax
from jax.experimental import pallas as pl
from jax.experimental.pallas import tpu as pltpu
from jax.sharding import PartitionSpec as P

BLOCK = 128
LOG2E = 1.4426950408889634
LANDED_FLOPS = 2 * 10**9


def contract(a, b, a_dim, b_dim):
    return lax.dot_general(a, b, (((a_dim,), (b_dim,)), ((), ())), preferred_element_type=jnp.float32)


def block_kernel(places_of, operand_count, first_call, last_call, slab_ref, me_ref, keys_ref, own_ref, prev_ref, lse_ref, delta_ref, *refs):
    qd_refs, refs = refs[:operand_count], refs[operand_count:]
    if not first_call:
        acc_in, refs = refs[0], refs[1:]
    dq_refs, refs = refs[: len(places_of)], refs[len(places_of) :]
    if last_call:
        own_out, prev_out, kv, kt, acc, cat_k, cat_v, cat_t = refs
    else:
        acc, kv, kt, cat_k, cat_v, cat_t = refs
    slab_blocks = own_ref.shape[0]
    heads = dq_refs[0].shape[1]
    select = keys_ref.shape[1]
    rows = heads * BLOCK
    head_dim = own_ref.shape[3]
    scale = 1.0 / math.sqrt(head_dim)
    first = slab_ref[0] * slab_blocks
    me = me_ref[0]

    def stage(c, _):
        for half, ref in ((0, prev_ref), (1, own_ref)):
            at = half * slab_blocks + c
            kv[0, at] = ref[c, 0]
            kv[1, at] = ref[c, 1]
            kt[at] = ref[c, 0].T
        return _

    lax.fori_loop(0, slab_blocks, stage, 0)
    acc[...] = jnp.zeros_like(acc) if first_call else acc_in[...]
    key_pos = lax.broadcasted_iota(jnp.int32, (BLOCK, rows), 0)
    query_pos = lax.broadcasted_iota(jnp.int32, (BLOCK, rows), 1) % BLOCK
    causal = key_pos <= query_pos

    def query_block(m, q_place, do_place, dq_ref, i, _):
        b = me ^ (2 * m + i)
        q, do = (qd_refs[x][i, at : at + heads].reshape(rows, head_dim) for x, at in (q_place, do_place))
        entries = [keys_ref[first + b, j] for j in range(select)]
        places = []
        for e in entries:
            local = e - first
            slot = jnp.where(local >= 0, slab_blocks + (local ^ me), (local + slab_blocks) ^ me)
            places.append(jnp.where(e >= 0, slot, 0))
        for j in range(select):
            cat_k[pl.ds(j * BLOCK, BLOCK)] = kv[0, places[j]]
            cat_v[pl.ds(j * BLOCK, BLOCK)] = kv[1, places[j]]
            cat_t[:, pl.ds(j * BLOCK, BLOCK)] = kt[places[j]]
        lanes = pl.ds(pl.multiple_of((first + b) * BLOCK, BLOCK), BLOCK)
        lse = jnp.concatenate([lse_ref[pl.ds(h, 1), lanes] for h in range(heads)], 1) * LOG2E
        delta = jnp.concatenate([delta_ref[pl.ds(h, 1), lanes] for h in range(heads)], 1)
        s = contract(cat_k[...], q, 1, 1)
        dp = contract(cat_v[...], do, 1, 1)
        p_parts = []
        for j in range(select):
            p = jnp.exp2(s[j * BLOCK : (j + 1) * BLOCK] * (scale * LOG2E) - lse)
            allowed = causal if j == 0 else entries[j] >= 0
            p_parts.append(jnp.where(allowed, p, 0.0))
        p = jnp.concatenate(p_parts, 0)
        ds = (p * (dp - delta)).astype(jnp.bfloat16)
        dv = contract(p.astype(jnp.bfloat16), do, 1, 0)
        dk = contract(ds, q, 1, 0)
        dqt = contract(cat_t[...], ds, 1, 0) * scale
        dq_ref[i] = dqt.T.astype(jnp.bfloat16).reshape(heads, BLOCK, head_dim)
        for j in range(select):
            part = slice(j * BLOCK, (j + 1) * BLOCK)
            acc[places[j], 0] += dk[part]
            acc[places[j], 1] += dv[part]
        return _

    for (m, q_place, do_place), dq_ref in zip(places_of, dq_refs):
        lax.fori_loop(0, 2, functools.partial(query_block, m, q_place, do_place, dq_ref), 0)

    if last_call:

        def finish(c, _):
            prev_out[c, 0] = (acc[c, 0] * scale).astype(prev_out.dtype)
            prev_out[c, 1] = acc[c, 1].astype(prev_out.dtype)
            own_out[c, 0] = acc[slab_blocks + c, 0] * scale
            own_out[c, 1] = acc[slab_blocks + c, 1]
            return _

        lax.fori_loop(0, slab_blocks, finish, 0)


def block_grads(parts, slab, me, block_keys, own, prev, lse, delta, acc, last_call):
    slab_blocks, _, _, head_dim = own.shape
    heads = lse.shape[0]
    select = block_keys.shape[1]
    smem = pl.BlockSpec(memory_space=pltpu.SMEM)
    vmem = pl.BlockSpec(memory_space=pltpu.VMEM)
    acc_shape = (2 * slab_blocks, 2, BLOCK, head_dim)
    wide = select * BLOCK
    macs = 2 * len(parts) * heads * select * 5 * BLOCK * BLOCK * head_dim
    arrays, places_of = [], []
    for m, *pair in parts:
        places = []
        for array, at in pair:
            if not any(array is x for x in arrays):
                arrays.append(array)
            places.append(([array is x for x in arrays].index(True), at))
        places_of.append((m, *places))
    operands = [own, prev, lse, delta, *arrays] + ([] if acc is None else [acc])
    out_shape = [jax.ShapeDtypeStruct((2, heads, BLOCK, head_dim), jnp.bfloat16) for _ in parts]
    scratch = [
        pltpu.VMEM((2, 2 * slab_blocks, BLOCK, head_dim), jnp.bfloat16),
        pltpu.VMEM((2 * slab_blocks, head_dim, BLOCK), jnp.bfloat16),
    ]
    if last_call:
        out_shape.append(jax.ShapeDtypeStruct(own.shape, jnp.float32))
        out_shape.append(jax.ShapeDtypeStruct(own.shape, jnp.bfloat16))
        scratch.append(pltpu.VMEM(acc_shape, jnp.float32))
    else:
        out_shape.append(jax.ShapeDtypeStruct(acc_shape, jnp.float32))
    return pl.pallas_call(
        functools.partial(block_kernel, places_of, len(arrays), acc is None, last_call),
        in_specs=[smem] * 3 + [vmem] * len(operands),
        out_specs=[vmem] * len(out_shape),
        out_shape=out_shape,
        scratch_shapes=scratch
        + [
            pltpu.VMEM((wide, head_dim), jnp.bfloat16),
            pltpu.VMEM((wide, head_dim), jnp.bfloat16),
            pltpu.VMEM((head_dim, wide), jnp.bfloat16),
        ],
        compiler_params=pltpu.CompilerParams(vmem_limit_bytes=40 * 1024 * 1024 if slab_blocks > 8 else 20 * 1024 * 1024),
        cost_estimate=pl.CostEstimate(flops=2 * macs, bytes_accessed=8 * 1024 * 1024, transcendentals=0),
    )(slab, me, block_keys, *operands)


def pack_kernel(fold_counts, me_ref, *refs):
    count = len(fold_counts)
    chips = refs[-1 - 2 * count - 1].shape[0]
    sources, pieces, give, refs = refs[:count], refs[count : count + chips], refs[count + chips], refs[count + chips + 1 :]
    by_token, by_head, sems = refs[:count], refs[count : 2 * count], refs[-1]
    devices = 2 * chips
    me = me_ref[0]
    copies = [pltpu.make_async_copy(sources[i], by_token[i], sems.at[i]) for i in range(count)]
    for copy in copies:
        copy.start()
    at = 0
    for copy, source, target, fold_count in zip(copies, by_token, by_head, fold_counts):
        copy.wait()
        target[...] = jnp.swapaxes(source[...], 0, 1)
        heads = target.shape[0] * fold_count // devices
        for m in range(chips):
            for out, j in ((pieces[m].at[0], 0), (give.at[m], 1)):
                device = me ^ (2 * m + j)
                out[at : at + heads] = target[pl.ds(device // fold_count * heads, heads)]
        at += heads


def packed(me, arrays, fold_counts, uly_count):
    tokens, _, head_dim = arrays[0].shape
    chips = uly_count // 2
    tiles = sum(x.shape[1] * fold_count for x, fold_count in zip(arrays, fold_counts)) // uly_count
    vmem = pl.BlockSpec(memory_space=pltpu.VMEM)
    shapes = [jax.ShapeDtypeStruct((2, tiles, tokens, head_dim), arrays[0].dtype)] * chips
    shapes.append(jax.ShapeDtypeStruct((chips, tiles, tokens, head_dim), arrays[0].dtype))
    *pieces, give = pl.pallas_call(
        functools.partial(pack_kernel, fold_counts),
        in_specs=[pl.BlockSpec(memory_space=pltpu.SMEM)] + [pl.BlockSpec(memory_space=pltpu.HBM)] * len(arrays),
        out_specs=[vmem] * len(shapes),
        out_shape=shapes,
        scratch_shapes=[pltpu.VMEM(x.shape, x.dtype) for x in arrays]
        + [pltpu.VMEM((x.shape[1], tokens, head_dim), x.dtype) for x in arrays]
        + [pltpu.SemaphoreType.DMA((len(arrays),))],
        compiler_params=pltpu.CompilerParams(vmem_limit_bytes=8 * 1024 * 1024),
    )(me, *[pltpu.with_memory_space_constraint(x, pltpu.HBM) for x in arrays])
    return pieces, give


def merge_kernel(chips, *refs):
    got, outs = refs[chips], refs[-chips:]
    for m in range(chips):
        outs[m][1] = got[m]


def merged(pieces, got, after):
    chips = len(pieces)
    vmem = pl.BlockSpec(memory_space=pltpu.VMEM)
    return pl.pallas_call(
        functools.partial(merge_kernel, chips),
        in_specs=[vmem] * (chips + 1) + [pl.BlockSpec(memory_space=pl.ANY)] * len(after),
        out_specs=[vmem] * chips,
        out_shape=[jax.ShapeDtypeStruct(x.shape, x.dtype) for x in pieces],
        input_output_aliases={m: m for m in range(chips)},
        compiler_params=pltpu.CompilerParams(vmem_limit_bytes=8 * 1024 * 1024),
    )(*pieces, got, *after)


def landed_kernel(piece, out):
    pass


def landed(piece):
    hold = pl.BlockSpec(memory_space=pl.ANY)
    return pl.pallas_call(
        landed_kernel,
        in_specs=[hold],
        out_specs=hold,
        out_shape=jax.ShapeDtypeStruct(piece.shape, piece.dtype),
        input_output_aliases={0: 0},
        cost_estimate=pl.CostEstimate(flops=LANDED_FLOPS, bytes_accessed=2**20, transcendentals=0),
    )(piece)


def join_kernel(*refs):
    *pieces, out = refs
    for m, piece in enumerate(pieces):
        out[2 * m : 2 * m + 2] = piece[...]


def joined(pieces):
    vmem = pl.BlockSpec(memory_space=pltpu.VMEM)
    return pl.pallas_call(
        join_kernel,
        in_specs=[vmem] * len(pieces),
        out_specs=vmem,
        out_shape=jax.ShapeDtypeStruct((2 * len(pieces), *pieces[0].shape[1:]), pieces[0].dtype),
        compiler_params=pltpu.CompilerParams(vmem_limit_bytes=16 * 1024 * 1024),
        cost_estimate=pl.CostEstimate(flops=2**20, bytes_accessed=2**20, transcendentals=0),
    )(*pieces)


def unpack_kernel(chips, fold_count, me_ref, *refs):
    here, (got, *refs) = refs[:chips], refs[chips:]
    count = (len(refs) - 1) // 3
    outs, by_head, by_token, sems = refs[:count], refs[count : 2 * count], refs[2 * count : 3 * count], refs[-1]
    me = me_ref[0]
    for k in range(2 * chips):
        device = me ^ k
        part = here[k // 2][0] if k % 2 == 0 else got[k // 2]
        heads = part.shape[0] // count
        for i in range(count):
            by_head[i][pl.ds(device * heads, heads)] = part[i * heads : (i + 1) * heads]
    copies = [pltpu.make_async_copy(by_token[i], outs[i], sems.at[i]) for i in range(count)]
    for i in range(count):
        whole = by_head[i][...]
        if fold_count > 1:
            whole = whole.reshape(-1, fold_count, *whole.shape[1:]).astype(jnp.float32).sum(1).astype(whole.dtype)
        by_token[i][...] = jnp.swapaxes(whole, 0, 1)
        copies[i].start()
    for copy in copies:
        copy.wait()


def unpacked(me, here, got, count, fold_count):
    chips, tiles, tokens, head_dim = got.shape
    devices = 2 * chips
    vmem = pl.BlockSpec(memory_space=pltpu.VMEM)
    heads = devices * tiles // count
    shape = (tokens, heads // fold_count, head_dim)
    return pl.pallas_call(
        functools.partial(unpack_kernel, chips, fold_count),
        in_specs=[pl.BlockSpec(memory_space=pltpu.SMEM)] + [vmem] * (chips + 1),
        out_specs=[pl.BlockSpec(memory_space=pltpu.HBM)] * count,
        out_shape=[jax.ShapeDtypeStruct(shape, got.dtype)] * count,
        scratch_shapes=[pltpu.VMEM((heads, tokens, head_dim), got.dtype)] * count
        + [pltpu.VMEM(shape, got.dtype)] * count
        + [pltpu.SemaphoreType.DMA((count,))],
        compiler_params=pltpu.CompilerParams(vmem_limit_bytes=16 * 1024 * 1024),
    )(me, *here, got)


def passed_along(block, axis, distance):
    devices = range(lax.axis_size(axis))
    return lax.ppermute(block, axis, [(i - distance, i) for i in devices if i - distance in devices])


def swapped(block, k):
    if k == 0:
        return block
    return lax.ppermute(block, "uly", [(i, i ^ k) for i in range(lax.axis_size("uly"))])


def sent_to_tokens(chunks, me, count, fold_count):
    here = [swapped(chunk, 2 * m) for m, chunk in enumerate(chunks)]
    got = swapped(jnp.stack([chunk[1] for chunk in here]), 1)
    return unpacked(me, here, got, count, fold_count)


def shards(queries, keys, values, grad_out, lse, delta, block_keys):
    uly_count = lax.axis_size("uly")
    head_total = queries.shape[1]
    fold_count = uly_count // keys.shape[1]
    heads = head_total // uly_count
    chips = uly_count // 2
    far = chips - 1
    me = lax.axis_index("uly").reshape(1)
    slab = lax.axis_index("blk").reshape(1)

    kv_pieces, give_kv = packed(me, [keys, values], [fold_count] * 2, uly_count)
    qd_pieces, give_qd = packed(me, [queries, grad_out], [1] * 2, uly_count)
    got_kv, got_qd = swapped(give_kv, 1), swapped(give_qd, 1)
    kv_pieces = [swapped(piece, 2 * m) for m, piece in enumerate(merged(kv_pieces, got_kv, []))]
    own = joined(kv_pieces)
    qd_pieces = [swapped(piece, 2 * m) for m, piece in enumerate(merged(qd_pieces, got_qd, kv_pieces[1:]))]
    qd_pieces[far] = landed(qd_pieces[far])
    prev = passed_along(own, "blk", 1)
    parts = [(m, (piece, 0), (piece, heads)) for m, piece in enumerate(qd_pieces)]

    grads = functools.partial(
        block_grads, slab=slab, me=me, block_keys=block_keys, own=own, prev=prev, lse=lse, delta=delta
    )
    order = [0] + list(range(far, 0, -1))
    early, late = order[: chips // 2], order[chips // 2 :]
    *dq_early, acc = grads([parts[m] for m in early], acc=None, last_call=False)
    *dq_late, own_grad, prev_grad = grads([parts[m] for m in late], acc=acc, last_call=True)
    back = passed_along(prev_grad, "blk", -1)
    kv_grad = (own_grad + back.astype(jnp.float32)).astype(jnp.bfloat16)
    kv_grad = [kv_grad[2 * m : 2 * m + 2] for m in range(chips)]
    dq = dict(zip(order, dq_early + dq_late))
    (grad_queries,) = sent_to_tokens([dq[m] for m in range(chips)], me, 1, 1)
    grad_keys, grad_values = sent_to_tokens(kv_grad, me, 2, fold_count)
    return grad_queries, grad_keys, grad_values


def solution(mesh):
    spread = P(("blk", "uly"), None, None)
    return jax.shard_map(
        shards,
        mesh=mesh,
        in_specs=(spread, spread, spread, spread, P("uly", None), P("uly", None), P()),
        out_specs=(spread, spread, spread),
        check_vma=False,
    )
```

```python
import functools
import math

import jax
import jax.numpy as jnp
from jax import lax
from jax.experimental import pallas as pl
from jax.experimental.pallas import tpu as pltpu
from jax.sharding import PartitionSpec as P

BLOCK = 128
LOG2E = 1.4426950408889634
FIRST, NEXT, LAST = range(3)
SHORT, ADD_COST = 2 * 10**9, 10**11


def contract(a, b, a_dim, b_dim):
    return lax.dot_general(a, b, (((a_dim,), (b_dim,)), ((), ())), preferred_element_type=jnp.float32)


def held(x):
    return pltpu.with_memory_space_constraint(x, pltpu.VMEM)


def block_kernel(blocks, out_count, half_count, operand_count, call, slab_ref, me_ref, keys_ref, lse_ref, delta_ref, *refs):
    qd_refs, refs = refs[:operand_count], refs[operand_count:]
    halves, refs = refs[:half_count], refs[half_count:]
    if call == FIRST:
        (own_ref, prev_ref), dq_refs, (kv, acc, cat_k, cat_v) = refs[:2], refs[2 : 2 + out_count], refs[2 + out_count :]
    else:
        (kv, acc_in), dq_refs, refs = refs[:2], refs[2 : 2 + out_count], refs[2 + out_count :]
        if call == LAST:
            own_out, *prev_out, acc, cat_k, cat_v = refs
        else:
            acc, cat_k, cat_v = refs
    for half, dq_ref in zip(halves, dq_refs):
        dq_ref[0] = half[0]
    slab_blocks = acc.shape[0] // 2
    heads = dq_refs[0].shape[1]
    select = keys_ref.shape[1]
    rows = heads * BLOCK
    head_dim = kv.shape[3]
    scale = 1.0 / math.sqrt(head_dim)
    first = slab_ref[0] * slab_blocks
    me = me_ref[0]
    if call != FIRST:
        acc[...] = acc_in[...]
    else:
        kv[:slab_blocks] = prev_ref[...]
        kv[slab_blocks:] = own_ref[...]
        acc[...] = jnp.zeros_like(acc)
    key_pos = lax.broadcasted_iota(jnp.int32, (BLOCK, rows), 0)
    query_pos = lax.broadcasted_iota(jnp.int32, (BLOCK, rows), 1) % BLOCK
    causal = key_pos <= query_pos

    def query_block(slot, operand, row, out, out_row):
        b = me ^ slot
        q = qd_refs[operand][row, :heads].reshape(rows, head_dim)
        do = qd_refs[operand][row, heads:].reshape(rows, head_dim)
        entries = [keys_ref[first + b, j] for j in range(select)]
        places = [jnp.where(e < first, 0, slab_blocks) + ((e - first) & (slab_blocks - 1) ^ me) for e in entries]
        for j, place in enumerate(places):
            cat_k[pl.ds(j * BLOCK, BLOCK)] = kv[place, 0]
            cat_v[pl.ds(j * BLOCK, BLOCK)] = kv[place, 1]
        lanes = pl.ds(pl.multiple_of((first + b) * BLOCK, BLOCK), BLOCK)
        lse = jnp.concatenate([lse_ref[pl.ds(h, 1), lanes] for h in range(heads)], 1) * LOG2E
        delta = jnp.concatenate([delta_ref[pl.ds(h, 1), lanes] for h in range(heads)], 1)
        s = contract(cat_k[...], q, 1, 1)
        dp = contract(cat_v[...], do, 1, 1)
        p_parts = []
        for j in range(select):
            p = jnp.exp2(s[j * BLOCK : (j + 1) * BLOCK] * (scale * LOG2E) - lse)
            allowed = causal if j == 0 else entries[j] >= 0
            p_parts.append(jnp.where(allowed, p, 0.0))
        p = jnp.concatenate(p_parts, 0)
        ds = (p * (dp - delta)).astype(jnp.bfloat16)
        dv = contract(p.astype(jnp.bfloat16), do, 1, 0)
        dk = contract(ds, q, 1, 0) * scale
        dq = contract(ds, cat_k[...], 0, 0) * scale
        dq_refs[out][out_row] = dq.astype(jnp.bfloat16).reshape(heads, BLOCK, head_dim)
        for j, place in enumerate(places):
            part = slice(j * BLOCK, (j + 1) * BLOCK)
            acc[place, 0] += dk[part]
            acc[place, 1] += dv[part]

    for block in blocks:
        query_block(*block)
    if call == LAST:
        at = 0
        for out in prev_out:
            out[...] = acc[at : at + out.shape[0]].astype(out.dtype)
            at += out.shape[0]
        own_out[...] = acc[slab_blocks:]


def block_grads(blocks, out_rows, slab, me, block_keys, lse, delta, pieces, halves, kept, call):
    slab_blocks = kept[0].shape[0] if call == FIRST else kept[0].shape[0] // 2
    head_dim = pieces[0].shape[3]
    heads = lse.shape[0]
    select = block_keys.shape[1]
    smem = pl.BlockSpec(memory_space=pltpu.SMEM)
    vmem = pl.BlockSpec(memory_space=pltpu.VMEM)
    wide = select * BLOCK
    macs = len(blocks) * heads * select * 5 * BLOCK * BLOCK * head_dim
    acc = jax.ShapeDtypeStruct((2 * slab_blocks, 2, BLOCK, head_dim), jnp.float32)
    out_shape = [jax.ShapeDtypeStruct((rows, heads, BLOCK, head_dim), jnp.bfloat16) for rows in out_rows]
    operands = [lse, delta, *pieces, *halves, *kept]
    if call == LAST:
        out_shape.append(jax.ShapeDtypeStruct((slab_blocks, 2, BLOCK, head_dim), jnp.float32))
        out_shape += [jax.ShapeDtypeStruct((count, 2, BLOCK, head_dim), jnp.bfloat16) for count in (2, slab_blocks - 4, 2)]
    elif call == FIRST:
        out_shape += [jax.ShapeDtypeStruct(acc.shape, jnp.bfloat16), acc]
    else:
        out_shape.append(acc)
    return pl.pallas_call(
        functools.partial(block_kernel, blocks, len(out_rows), len(halves), len(pieces), call),
        in_specs=[smem] * 3 + [vmem] * len(operands),
        out_specs=[vmem] * len(out_shape),
        out_shape=out_shape,
        scratch_shapes=[pltpu.VMEM(acc.shape, acc.dtype)] * (call == LAST) + [pltpu.VMEM((wide, head_dim), jnp.bfloat16)] * 2,
        compiler_params=pltpu.CompilerParams(vmem_limit_bytes=32 * 1024 * 1024 if slab_blocks > 8 else 16 * 1024 * 1024),
        cost_estimate=pl.CostEstimate(flops=2 * macs, bytes_accessed=8 * 1024 * 1024, transcendentals=0),
    )(slab, me, block_keys, *operands)


def pack_kernel(fold_counts, after_count, me_ref, *refs):
    count = len(fold_counts)
    chips = refs[-1 - 2 * count - 1].shape[0]
    sources, refs = refs[:count], refs[count + after_count :]
    pieces, give, refs = refs[:chips], refs[chips], refs[chips + 1 :]
    by_token, by_head, sems = refs[:count], refs[count : 2 * count], refs[-1]
    devices = 2 * chips
    me = me_ref[0]
    copies = [pltpu.make_async_copy(sources[i], by_token[i], sems.at[i]) for i in range(count)]
    for copy in copies:
        copy.start()
    at = 0
    for copy, source, target, fold_count in zip(copies, by_token, by_head, fold_counts):
        copy.wait()
        target[...] = jnp.swapaxes(source[...], 0, 1)
        heads = target.shape[0] * fold_count // devices
        for m in range(chips):
            for out, j in ((pieces[m].at[0], 0), (give.at[m], 1)):
                device = me ^ (2 * m + j)
                out[at : at + heads] = target[pl.ds(device // fold_count * heads, heads)]
        at += heads


def packed(me, arrays, fold_counts, uly_count, whole, after):
    tokens, _, head_dim = arrays[0].shape
    chips = uly_count // 2
    tiles = sum(x.shape[1] * fold_count for x, fold_count in zip(arrays, fold_counts)) // uly_count
    vmem = pl.BlockSpec(memory_space=pltpu.VMEM)
    shapes = [jax.ShapeDtypeStruct((2 if m in whole else 1, tiles, tokens, head_dim), arrays[0].dtype) for m in range(chips)]
    shapes.append(jax.ShapeDtypeStruct((chips, tiles, tokens, head_dim), arrays[0].dtype))
    *pieces, give = pl.pallas_call(
        functools.partial(pack_kernel, fold_counts, len(after)),
        in_specs=[pl.BlockSpec(memory_space=pltpu.SMEM)] + [pl.BlockSpec(memory_space=pltpu.HBM)] * len(arrays) + [pl.BlockSpec(memory_space=pl.ANY)] * len(after),
        out_specs=[vmem] * len(shapes),
        out_shape=shapes,
        scratch_shapes=[pltpu.VMEM(x.shape, x.dtype) for x in arrays]
        + [pltpu.VMEM((x.shape[1], tokens, head_dim), x.dtype) for x in arrays]
        + [pltpu.SemaphoreType.DMA((len(arrays),))],
        compiler_params=pltpu.CompilerParams(vmem_limit_bytes=8 * 1024 * 1024),
    )(me, *[pltpu.with_memory_space_constraint(x, pltpu.HBM) for x in arrays], *after)
    return pieces, give


def merge_kernel(whole, chips, count, *refs):
    got, outs = refs[len(whole)], refs[-count:]
    for m, out in zip(whole, outs):
        out[1] = got[m]
    for m, out in zip([m for m in range(chips) if m not in whole], outs[len(whole) :]):
        out[0] = got[m]


def merged(pieces, whole, got, after):
    chips = got.shape[0]
    apart = chips - len(whole)
    vmem = pl.BlockSpec(memory_space=pltpu.VMEM)
    shapes = [jax.ShapeDtypeStruct(pieces[m].shape, got.dtype) for m in whole]
    shapes += [jax.ShapeDtypeStruct((1, *got.shape[1:]), got.dtype)] * apart
    return pl.pallas_call(
        functools.partial(merge_kernel, whole, chips, len(shapes)),
        in_specs=[vmem] * (len(whole) + 1) + [pl.BlockSpec(memory_space=pl.ANY)] * len(after),
        out_specs=[vmem] * chips,
        out_shape=shapes,
        input_output_aliases={i: i for i in range(len(whole))},
        compiler_params=pltpu.CompilerParams(vmem_limit_bytes=8 * 1024 * 1024),
    )(*[held(pieces[m]) for m in whole], got, *after)


def landed_kernel(*refs):
    pass


def landed(piece, after, flops):
    hold = pl.BlockSpec(memory_space=pl.ANY)
    return pl.pallas_call(
        landed_kernel,
        in_specs=[hold] * (1 + len(after)),
        out_specs=hold,
        out_shape=jax.ShapeDtypeStruct(piece.shape, piece.dtype),
        input_output_aliases={0: 0},
        cost_estimate=pl.CostEstimate(flops=flops, bytes_accessed=2**20, transcendentals=0),
    )(piece, *after)


def join_kernel(*refs):
    *pieces, out = refs
    for m, piece in enumerate(pieces):
        out[2 * m : 2 * m + 2] = piece[...]


def joined(pieces):
    vmem = pl.BlockSpec(memory_space=pltpu.VMEM)
    return pl.pallas_call(
        join_kernel,
        in_specs=[vmem] * len(pieces),
        out_specs=vmem,
        out_shape=jax.ShapeDtypeStruct((2 * len(pieces), *pieces[0].shape[1:]), pieces[0].dtype),
        compiler_params=pltpu.CompilerParams(vmem_limit_bytes=16 * 1024 * 1024),
        cost_estimate=pl.CostEstimate(flops=2**20, bytes_accessed=2**20, transcendentals=0),
    )(*pieces)


def add_kernel(first, after_count, own, back, *refs):
    for i, out in enumerate(refs[after_count:]):
        rows = slice(2 * (first + i), 2 * (first + i) + 2)
        out[...] = (own[rows] + back[2 * i : 2 * i + 2].astype(jnp.float32)).astype(out.dtype)


def added(first, own, back, after):
    vmem = pl.BlockSpec(memory_space=pltpu.VMEM)
    count = back.shape[0] // 2
    return pl.pallas_call(
        functools.partial(add_kernel, first, len(after)),
        in_specs=[vmem] * 2 + [vmem if x.ndim == 4 else pl.BlockSpec(memory_space=pltpu.HBM) for x in after],
        out_specs=[vmem] * count,
        out_shape=[jax.ShapeDtypeStruct((2, *back.shape[1:]), back.dtype)] * count,
        compiler_params=pltpu.CompilerParams(vmem_limit_bytes=8 * 1024 * 1024),
        cost_estimate=pl.CostEstimate(flops=ADD_COST, bytes_accessed=2**20, transcendentals=0),
    )(own, back, *[x if x.ndim == 4 else pltpu.with_memory_space_constraint(x, pltpu.HBM) for x in after])


def collect_kernel(chips, *refs):
    for m in range(chips):
        refs[-1][m] = refs[m][1]


def collected(chunks, after):
    vmem = pl.BlockSpec(memory_space=pltpu.VMEM)
    return pl.pallas_call(
        functools.partial(collect_kernel, len(chunks)),
        in_specs=[vmem] * len(chunks) + [pl.BlockSpec(memory_space=pl.ANY)] * len(after),
        out_specs=vmem,
        out_shape=jax.ShapeDtypeStruct((len(chunks), *chunks[0].shape[1:]), chunks[0].dtype),
        compiler_params=pltpu.CompilerParams(vmem_limit_bytes=8 * 1024 * 1024),
    )(*chunks, *after)


def unpack_kernel(chips, fold_count, me_ref, *refs):
    here, (got, *refs) = refs[:chips], refs[chips:]
    count = (len(refs) - 1) // 3
    outs, by_head, by_token, sems = refs[:count], refs[count : 2 * count], refs[2 * count : 3 * count], refs[-1]
    me = me_ref[0]
    for k in range(2 * chips):
        device = me ^ k
        part = here[k // 2][0] if k % 2 == 0 else got[k // 2]
        heads = part.shape[0] // count
        for i in range(count):
            by_head[i][pl.ds(device * heads, heads)] = part[i * heads : (i + 1) * heads]
    copies = [pltpu.make_async_copy(by_token[i], outs[i], sems.at[i]) for i in range(count)]
    for i in range(count):
        whole = by_head[i][...]
        if fold_count > 1:
            whole = whole.reshape(-1, fold_count, *whole.shape[1:]).astype(jnp.float32).sum(1).astype(whole.dtype)
        by_token[i][...] = jnp.swapaxes(whole, 0, 1)
        copies[i].start()
    for copy in copies:
        copy.wait()


def unpacked(me, here, got, count, fold_count):
    chips, tiles, tokens, head_dim = got.shape
    devices = 2 * chips
    vmem = pl.BlockSpec(memory_space=pltpu.VMEM)
    heads = devices * tiles // count
    shape = (tokens, heads // fold_count, head_dim)
    return pl.pallas_call(
        functools.partial(unpack_kernel, chips, fold_count),
        in_specs=[pl.BlockSpec(memory_space=pltpu.SMEM)] + [vmem] * (chips + 1),
        out_specs=[pl.BlockSpec(memory_space=pltpu.HBM)] * count,
        out_shape=[jax.ShapeDtypeStruct(shape, got.dtype)] * count,
        scratch_shapes=[pltpu.VMEM((heads, tokens, head_dim), got.dtype)] * count
        + [pltpu.VMEM(shape, got.dtype)] * count
        + [pltpu.SemaphoreType.DMA((count,))],
        compiler_params=pltpu.CompilerParams(vmem_limit_bytes=16 * 1024 * 1024),
    )(me, *here, got)


def passed_along(block, axis, distance):
    devices = range(lax.axis_size(axis))
    return lax.ppermute(block, axis, [(i - distance, i) for i in devices if i - distance in devices])


def swapped(block, k):
    if k == 0:
        return block
    return lax.ppermute(block, "uly", [(i, i ^ k) for i in range(lax.axis_size("uly"))])


def shards(queries, keys, values, grad_out, lse, delta, block_keys):
    uly_count = lax.axis_size("uly")
    head_total = queries.shape[1]
    fold_count = uly_count // keys.shape[1]
    heads = head_total // uly_count
    chips = uly_count // 2
    far = chips - 1
    me = lax.axis_index("uly").reshape(1)
    slab = lax.axis_index("blk").reshape(1)

    every, ends, mids = list(range(chips)), [0, far], list(range(1, far))
    kv_pieces, give_kv = packed(me, [keys, values], [fold_count] * 2, uly_count, every, [])
    merged_kv = merged(kv_pieces, every, swapped(give_kv, 1), [])
    kv_pieces = [swapped(piece, 2 * m) for m, piece in enumerate(merged_kv)]
    own = joined(kv_pieces)
    qd_pieces, give_qd = packed(me, [queries, grad_out], [1] * 2, uly_count, ends, merged_kv[:1])
    qd_here, qd_far, *seconds = merged(qd_pieces, ends, swapped(give_qd, 1), kv_pieces[1:])
    qd_far = landed(swapped(qd_far, 2 * far), [], SHORT)
    firsts = [swapped(qd_pieces[m], 2 * m) for m in mids]
    seconds = [swapped(piece, 2 * m) for m, piece in zip(mids, seconds)]
    prev = passed_along(own, "blk", 1)

    grads = functools.partial(block_grads, slab=slab, me=me, block_keys=block_keys, lse=lse, delta=delta)
    blocks = [(2 * m + i, operand, i, operand, i) for operand, m in enumerate(ends) for i in range(2)]
    dq_here, dq_far, kv, acc = grads(blocks, [2, 2], pieces=[qd_here, qd_far], halves=[], kept=[own, prev], call=FIRST)
    blocks = [(2 * m, i, 0, i, 0) for i, m in enumerate(mids)]
    *halves, acc = grads(blocks, [1] * len(mids), pieces=firsts, halves=[], kept=[kv, acc], call=NEXT)
    blocks = [(2 * m + 1, i, 0, i, 1) for i, m in enumerate(mids)]
    outs = grads(blocks, [2] * len(mids), pieces=seconds, halves=halves, kept=[kv, acc], call=LAST)
    *dq_mid, own_grad, prev_here, prev_mid, prev_far = outs
    dq = [swapped(x, 2 * m) for m, x in enumerate([dq_here, *dq_mid, dq_far])]

    def back_added(part, first, after):
        total = added(first, own_grad, passed_along(part, "blk", -1), after)
        return [swapped(x, 2 * (first + i)) for i, x in enumerate(total)]

    kv_far = back_added(prev_far, far, [dq[far]])
    (grad_queries,) = unpacked(me, dq, swapped(collected(dq, []), 1), 1, 1)
    kv_mid = back_added(prev_mid, 1, dq[1:far] + kv_far)
    kv_here = back_added(prev_here, 0, kv_mid + [grad_queries])
    kv_grad = kv_here + kv_mid + kv_far
    got_kv = swapped(collected(kv_grad, []), 1)
    grad_keys, grad_values = unpacked(me, kv_grad, got_kv, 2, fold_count)
    return grad_queries, grad_keys, grad_values


def solution(mesh):
    spread = P(("blk", "uly"), None, None)
    return jax.shard_map(
        shards,
        mesh=mesh,
        in_specs=(spread, spread, spread, spread, P("uly", None), P("uly", None), P()),
        out_specs=(spread, spread, spread),
        check_vma=False,
    )
```

```python
import functools
import math

import jax
import jax.numpy as jnp
from jax import lax
from jax.experimental import pallas as pl
from jax.experimental.pallas import tpu as pltpu
from jax.sharding import PartitionSpec as P

BLOCK = 128
LOG2E = 1.4426950408889634
FIRST, NEXT, LAST = range(3)
SHORT, ADD_COST = 2 * 10**9, 10**11


def contract(a, b, a_dim, b_dim):
    return lax.dot_general(a, b, (((a_dim,), (b_dim,)), ((), ())), preferred_element_type=jnp.float32)


def held(x):
    return pltpu.with_memory_space_constraint(x, pltpu.VMEM)


def block_kernel(blocks, out_count, half_count, operand_count, call, slab_ref, me_ref, keys_ref, lse_ref, delta_ref, *refs):
    qd_refs, refs = refs[:operand_count], refs[operand_count:]
    halves, refs = refs[:half_count], refs[half_count:]
    if call == FIRST:
        (own_ref, prev_ref), dq_refs, (kv, acc, cat_k, cat_v) = refs[:2], refs[2 : 2 + out_count], refs[2 + out_count :]
    else:
        (kv, acc_in), dq_refs, refs = refs[:2], refs[2 : 2 + out_count], refs[2 + out_count :]
        if call == LAST:
            own_out, *prev_out, acc, cat_k, cat_v = refs
        else:
            acc, cat_k, cat_v = refs
    for half, dq_ref in zip(halves, dq_refs):
        dq_ref[0] = half[0]
    slab_blocks = acc.shape[0] // 2
    heads = dq_refs[0].shape[1]
    select = keys_ref.shape[1]
    rows = heads * BLOCK
    head_dim = kv.shape[3]
    scale = 1.0 / math.sqrt(head_dim)
    first = slab_ref[0] * slab_blocks
    me = me_ref[0]
    if call != FIRST:
        acc[...] = acc_in[...]
    else:
        kv[:slab_blocks] = prev_ref[...]
        kv[slab_blocks:] = own_ref[...]
        acc[...] = jnp.zeros_like(acc)
    key_pos = lax.broadcasted_iota(jnp.int32, (BLOCK, rows), 0)
    query_pos = lax.broadcasted_iota(jnp.int32, (BLOCK, rows), 1) % BLOCK
    causal = key_pos <= query_pos

    def query_block(slot, operand, row, out, out_row):
        b = me ^ slot
        q = qd_refs[operand][row, :heads].reshape(rows, head_dim)
        do = qd_refs[operand][row, heads:].reshape(rows, head_dim)
        entries = [keys_ref[first + b, j] for j in range(select)]
        places = [jnp.where(e < first, 0, slab_blocks) + ((e - first) & (slab_blocks - 1) ^ me) for e in entries]
        for j, place in enumerate(places):
            cat_k[pl.ds(j * BLOCK, BLOCK)] = kv[place, 0]
            cat_v[pl.ds(j * BLOCK, BLOCK)] = kv[place, 1]
        lanes = pl.ds(pl.multiple_of((first + b) * BLOCK, BLOCK), BLOCK)
        lse = jnp.concatenate([lse_ref[pl.ds(h, 1), lanes] for h in range(heads)], 1) * LOG2E
        delta = jnp.concatenate([delta_ref[pl.ds(h, 1), lanes] for h in range(heads)], 1)
        s = contract(cat_k[...], q, 1, 1)
        dp = contract(cat_v[...], do, 1, 1)
        p_parts = []
        for j in range(select):
            p = jnp.exp2(s[j * BLOCK : (j + 1) * BLOCK] * (scale * LOG2E) - lse)
            allowed = causal if j == 0 else entries[j] >= 0
            p_parts.append(jnp.where(allowed, p, 0.0))
        p = jnp.concatenate(p_parts, 0)
        ds = (p * (dp - delta)).astype(jnp.bfloat16)
        dv = contract(p.astype(jnp.bfloat16), do, 1, 0)
        dk = contract(ds, q, 1, 0) * scale
        dq = contract(ds, cat_k[...], 0, 0) * scale
        dq_refs[out][out_row] = dq.astype(jnp.bfloat16).reshape(heads, BLOCK, head_dim)
        for j, place in enumerate(places):
            part = slice(j * BLOCK, (j + 1) * BLOCK)
            acc[place, 0] += dk[part]
            acc[place, 1] += dv[part]

    for block in blocks:
        query_block(*block)
    if call == LAST:
        at = 0
        for out in prev_out:
            out[...] = acc[at : at + out.shape[0]].astype(out.dtype)
            at += out.shape[0]
        own_out[...] = acc[slab_blocks:]


def block_grads(blocks, out_rows, slab, me, block_keys, lse, delta, pieces, halves, kept, call):
    slab_blocks = kept[0].shape[0] if call == FIRST else kept[0].shape[0] // 2
    head_dim = pieces[0].shape[3]
    heads = lse.shape[0]
    select = block_keys.shape[1]
    smem = pl.BlockSpec(memory_space=pltpu.SMEM)
    vmem = pl.BlockSpec(memory_space=pltpu.VMEM)
    wide = select * BLOCK
    macs = len(blocks) * heads * select * 5 * BLOCK * BLOCK * head_dim
    acc = jax.ShapeDtypeStruct((2 * slab_blocks, 2, BLOCK, head_dim), jnp.float32)
    out_shape = [jax.ShapeDtypeStruct((rows, heads, BLOCK, head_dim), jnp.bfloat16) for rows in out_rows]
    operands = [lse, delta, *pieces, *halves, *kept]
    if call == LAST:
        out_shape.append(jax.ShapeDtypeStruct((slab_blocks, 2, BLOCK, head_dim), jnp.float32))
        out_shape += [jax.ShapeDtypeStruct((count, 2, BLOCK, head_dim), jnp.bfloat16) for count in (2, slab_blocks - 4, 2)]
    elif call == FIRST:
        out_shape += [jax.ShapeDtypeStruct(acc.shape, jnp.bfloat16), acc]
    else:
        out_shape.append(acc)
    return pl.pallas_call(
        functools.partial(block_kernel, blocks, len(out_rows), len(halves), len(pieces), call),
        in_specs=[smem] * 3 + [vmem] * len(operands),
        out_specs=[vmem] * len(out_shape),
        out_shape=out_shape,
        scratch_shapes=[pltpu.VMEM(acc.shape, acc.dtype)] * (call == LAST) + [pltpu.VMEM((wide, head_dim), jnp.bfloat16)] * 2,
        compiler_params=pltpu.CompilerParams(vmem_limit_bytes=32 * 1024 * 1024 if slab_blocks > 8 else 16 * 1024 * 1024),
        cost_estimate=pl.CostEstimate(flops=2 * macs, bytes_accessed=8 * 1024 * 1024, transcendentals=0),
    )(slab, me, block_keys, *operands)


def pack_kernel(devices, fold_counts, kept, given, after_count, me_ref, *refs):
    count = len(fold_counts)
    sources, refs = refs[:count], refs[count + after_count :]
    pieces, gives, refs = refs[: len(kept)], refs[len(kept) : len(kept) + len(given)], refs[len(kept) + len(given) :]
    by_token, by_head, sems = refs[:count], refs[count : 2 * count], refs[-1]
    me = me_ref[0]
    targets = [(piece.at[0], 2 * m) for piece, m in zip(pieces, kept)]
    targets += [(give.at[i], 2 * m + 1) for give, group in zip(gives, given) for i, m in enumerate(group)]
    copies = [pltpu.make_async_copy(sources[i], by_token[i], sems.at[i]) for i in range(count)]
    for copy in copies:
        copy.start()
    at = 0
    for copy, source, target, fold_count in zip(copies, by_token, by_head, fold_counts):
        copy.wait()
        target[...] = jnp.swapaxes(source[...], 0, 1)
        heads = target.shape[0] * fold_count // devices
        for out, slot in targets:
            device = me ^ slot
            out[at : at + heads] = target[pl.ds(device // fold_count * heads, heads)]
        at += heads


def packed(me, arrays, fold_counts, uly_count, kept, rows, given, after):
    tokens, _, head_dim = arrays[0].shape
    tiles = sum(x.shape[1] * fold_count for x, fold_count in zip(arrays, fold_counts)) // uly_count
    vmem = pl.BlockSpec(memory_space=pltpu.VMEM)
    counts = [rows] * len(kept) + [len(group) for group in given]
    shapes = [jax.ShapeDtypeStruct((count, tiles, tokens, head_dim), arrays[0].dtype) for count in counts]
    return pl.pallas_call(
        functools.partial(pack_kernel, uly_count, fold_counts, kept, given, len(after)),
        in_specs=[pl.BlockSpec(memory_space=pltpu.SMEM)]
        + [pl.BlockSpec(memory_space=pltpu.HBM)] * len(arrays)
        + [pl.BlockSpec(memory_space=pl.ANY)] * len(after),
        out_specs=[vmem] * len(shapes),
        out_shape=shapes,
        scratch_shapes=[pltpu.VMEM(x.shape, x.dtype) for x in arrays]
        + [pltpu.VMEM((x.shape[1], tokens, head_dim), x.dtype) for x in arrays]
        + [pltpu.SemaphoreType.DMA((len(arrays),))],
        compiler_params=pltpu.CompilerParams(vmem_limit_bytes=8 * 1024 * 1024),
    )(me, *[pltpu.with_memory_space_constraint(x, pltpu.HBM) for x in arrays], *after)


def merge_kernel(count, *refs):
    got, outs = refs[count], refs[-count:]
    for i, out in enumerate(outs):
        out[1] = got[i]


def merged(pieces, got, after):
    count = len(pieces)
    vmem = pl.BlockSpec(memory_space=pltpu.VMEM)
    return pl.pallas_call(
        functools.partial(merge_kernel, count),
        in_specs=[vmem] * (count + 1) + [pl.BlockSpec(memory_space=pl.ANY)] * len(after),
        out_specs=[vmem] * count,
        out_shape=[jax.ShapeDtypeStruct(x.shape, x.dtype) for x in pieces],
        input_output_aliases={i: i for i in range(count)},
        compiler_params=pltpu.CompilerParams(vmem_limit_bytes=8 * 1024 * 1024),
    )(*map(held, pieces), got, *after)


def landed_kernel(*refs):
    pass


def landed(piece, after, flops):
    hold = pl.BlockSpec(memory_space=pl.ANY)
    return pl.pallas_call(
        landed_kernel,
        in_specs=[hold] * (1 + len(after)),
        out_specs=hold,
        out_shape=jax.ShapeDtypeStruct(piece.shape, piece.dtype),
        input_output_aliases={0: 0},
        cost_estimate=pl.CostEstimate(flops=flops, bytes_accessed=2**20, transcendentals=0),
    )(piece, *after)


def join_kernel(*refs):
    *pieces, out = refs
    for m, piece in enumerate(pieces):
        out[2 * m : 2 * m + 2] = piece[...]


def joined(pieces):
    vmem = pl.BlockSpec(memory_space=pltpu.VMEM)
    return pl.pallas_call(
        join_kernel,
        in_specs=[vmem] * len(pieces),
        out_specs=vmem,
        out_shape=jax.ShapeDtypeStruct((2 * len(pieces), *pieces[0].shape[1:]), pieces[0].dtype),
        compiler_params=pltpu.CompilerParams(vmem_limit_bytes=16 * 1024 * 1024),
        cost_estimate=pl.CostEstimate(flops=2**20, bytes_accessed=2**20, transcendentals=0),
    )(*pieces)


def add_kernel(first, after_count, own, back, *refs):
    for i, out in enumerate(refs[after_count:]):
        rows = slice(2 * (first + i), 2 * (first + i) + 2)
        out[...] = (own[rows] + back[2 * i : 2 * i + 2].astype(jnp.float32)).astype(out.dtype)


def added(first, own, back, after):
    vmem = pl.BlockSpec(memory_space=pltpu.VMEM)
    count = back.shape[0] // 2
    return pl.pallas_call(
        functools.partial(add_kernel, first, len(after)),
        in_specs=[vmem] * 2 + [vmem if x.ndim == 4 else pl.BlockSpec(memory_space=pltpu.HBM) for x in after],
        out_specs=[vmem] * count,
        out_shape=[jax.ShapeDtypeStruct((2, *back.shape[1:]), back.dtype)] * count,
        compiler_params=pltpu.CompilerParams(vmem_limit_bytes=8 * 1024 * 1024),
        cost_estimate=pl.CostEstimate(flops=ADD_COST, bytes_accessed=2**20, transcendentals=0),
    )(own, back, *[x if x.ndim == 4 else pltpu.with_memory_space_constraint(x, pltpu.HBM) for x in after])


def collect_kernel(chips, *refs):
    for m in range(chips):
        refs[-1][m] = refs[m][1]


def collected(chunks, after):
    vmem = pl.BlockSpec(memory_space=pltpu.VMEM)
    return pl.pallas_call(
        functools.partial(collect_kernel, len(chunks)),
        in_specs=[vmem] * len(chunks) + [pl.BlockSpec(memory_space=pl.ANY)] * len(after),
        out_specs=vmem,
        out_shape=jax.ShapeDtypeStruct((len(chunks), *chunks[0].shape[1:]), chunks[0].dtype),
        compiler_params=pltpu.CompilerParams(vmem_limit_bytes=8 * 1024 * 1024),
    )(*chunks, *after)


def unpack_kernel(chips, fold_count, me_ref, *refs):
    here, (got, *refs) = refs[:chips], refs[chips:]
    count = (len(refs) - 1) // 3
    outs, by_head, by_token, sems = refs[:count], refs[count : 2 * count], refs[2 * count : 3 * count], refs[-1]
    me = me_ref[0]
    for k in range(2 * chips):
        device = me ^ k
        part = here[k // 2][0] if k % 2 == 0 else got[k // 2]
        heads = part.shape[0] // count
        for i in range(count):
            by_head[i][pl.ds(device * heads, heads)] = part[i * heads : (i + 1) * heads]
    copies = [pltpu.make_async_copy(by_token[i], outs[i], sems.at[i]) for i in range(count)]
    for i in range(count):
        whole = by_head[i][...]
        if fold_count > 1:
            whole = whole.reshape(-1, fold_count, *whole.shape[1:]).astype(jnp.float32).sum(1).astype(whole.dtype)
        by_token[i][...] = jnp.swapaxes(whole, 0, 1)
        copies[i].start()
    for copy in copies:
        copy.wait()


def unpacked(me, here, got, count, fold_count):
    chips, tiles, tokens, head_dim = got.shape
    devices = 2 * chips
    vmem = pl.BlockSpec(memory_space=pltpu.VMEM)
    heads = devices * tiles // count
    shape = (tokens, heads // fold_count, head_dim)
    return pl.pallas_call(
        functools.partial(unpack_kernel, chips, fold_count),
        in_specs=[pl.BlockSpec(memory_space=pltpu.SMEM)] + [vmem] * (chips + 1),
        out_specs=[pl.BlockSpec(memory_space=pltpu.HBM)] * count,
        out_shape=[jax.ShapeDtypeStruct(shape, got.dtype)] * count,
        scratch_shapes=[pltpu.VMEM((heads, tokens, head_dim), got.dtype)] * count
        + [pltpu.VMEM(shape, got.dtype)] * count
        + [pltpu.SemaphoreType.DMA((count,))],
        compiler_params=pltpu.CompilerParams(vmem_limit_bytes=16 * 1024 * 1024),
    )(me, *here, got)


def passed_along(block, axis, distance):
    devices = range(lax.axis_size(axis))
    return lax.ppermute(block, axis, [(i - distance, i) for i in devices if i - distance in devices])


def swapped(block, k):
    if k == 0:
        return block
    return lax.ppermute(block, "uly", [(i, i ^ k) for i in range(lax.axis_size("uly"))])


def shards(queries, keys, values, grad_out, lse, delta, block_keys):
    uly_count = lax.axis_size("uly")
    head_total = queries.shape[1]
    fold_count = uly_count // keys.shape[1]
    heads = head_total // uly_count
    chips = uly_count // 2
    far = chips - 1
    me = lax.axis_index("uly").reshape(1)
    slab = lax.axis_index("blk").reshape(1)

    every, ends, mids = list(range(chips)), [0, far], list(range(1, far))
    *kv_pieces, give_kv = packed(me, [keys, values], [fold_count] * 2, uly_count, every, 2, [every], [])
    merged_kv = merged(kv_pieces, swapped(give_kv, 1), [])
    kv_pieces = [swapped(piece, 2 * m) for m, piece in enumerate(merged_kv)]
    own = joined(kv_pieces)
    pack = functools.partial(packed, me, [queries, grad_out], [1] * 2, uly_count)
    *qd_ends, give_ends, give_mids = pack(ends, 2, [ends, mids], merged_kv[:1])
    qd_here, qd_far = merged(qd_ends, swapped(give_ends, 1), kv_pieces[1:])
    qd_far = landed(swapped(qd_far, 2 * far), [], SHORT)
    got_mids = swapped(give_mids, 1)
    firsts = [swapped(piece, 2 * m) for m, piece in zip(mids, pack(mids, 1, [], [own]))]
    seconds = [swapped(got_mids[i : i + 1], 2 * m) for i, m in enumerate(mids)]
    prev = passed_along(own, "blk", 1)

    grads = functools.partial(block_grads, slab=slab, me=me, block_keys=block_keys, lse=lse, delta=delta)
    blocks = [(2 * m + i, operand, i, operand, i) for operand, m in enumerate(ends) for i in range(2)]
    dq_here, dq_far, kv, acc = grads(blocks, [2, 2], pieces=[qd_here, qd_far], halves=[], kept=[own, prev], call=FIRST)
    blocks = [(2 * m, i, 0, i, 0) for i, m in enumerate(mids)]
    *halves, acc = grads(blocks, [1] * len(mids), pieces=firsts, halves=[], kept=[kv, acc], call=NEXT)
    blocks = [(2 * m + 1, i, 0, i, 1) for i, m in enumerate(mids)]
    outs = grads(blocks, [2] * len(mids), pieces=seconds, halves=halves, kept=[kv, acc], call=LAST)
    *dq_mid, own_grad, prev_here, prev_mid, prev_far = outs
    dq = [swapped(x, 2 * m) for m, x in enumerate([dq_here, *dq_mid, dq_far])]

    def back_added(part, first, after):
        total = added(first, own_grad, passed_along(part, "blk", -1), after)
        return [swapped(x, 2 * (first + i)) for i, x in enumerate(total)]

    kv_far = back_added(prev_far, far, [dq[far]])
    (grad_queries,) = unpacked(me, dq, swapped(collected(dq, []), 1), 1, 1)
    kv_mid = back_added(prev_mid, 1, dq[1:far] + kv_far)
    kv_here = back_added(prev_here, 0, kv_mid + [grad_queries])
    kv_grad = kv_here + kv_mid + kv_far
    got_kv = swapped(collected(kv_grad, []), 1)
    grad_keys, grad_values = unpacked(me, kv_grad, got_kv, 2, fold_count)
    return grad_queries, grad_keys, grad_values


def solution(mesh):
    spread = P(("blk", "uly"), None, None)
    return jax.shard_map(
        shards,
        mesh=mesh,
        in_specs=(spread, spread, spread, spread, P("uly", None), P("uly", None), P()),
        out_specs=(spread, spread, spread),
        check_vma=False,
    )
```

```python
import functools
import math

import jax
import jax.numpy as jnp
from jax import lax
from jax.experimental import pallas as pl
from jax.experimental.pallas import tpu as pltpu
from jax.sharding import PartitionSpec as P

BLOCK = 128
LOG2E = 1.4426950408889634
FIRST, NEXT, LAST = range(3)
SHORT, JOIN_COST, ADD_COST = 2 * 10**9, 10**10, 10**11


def contract(a, b, a_dim, b_dim):
    return lax.dot_general(a, b, (((a_dim,), (b_dim,)), ((), ())), preferred_element_type=jnp.float32)


def held(x):
    return pltpu.with_memory_space_constraint(x, pltpu.VMEM)


def block_kernel(blocks, out_count, half_count, operand_count, call, slab_ref, me_ref, keys_ref, lse_ref, delta_ref, *refs):
    qd_refs, refs = refs[:operand_count], refs[operand_count:]
    halves, refs = refs[:half_count], refs[half_count:]
    if call == FIRST:
        (own_ref, prev_ref), dq_refs, (kv, acc, cat_k, cat_v) = refs[:2], refs[2 : 2 + out_count], refs[2 + out_count :]
    else:
        (kv, acc_in), dq_refs, refs = refs[:2], refs[2 : 2 + out_count], refs[2 + out_count :]
        if call == LAST:
            own_out, *prev_out, acc, cat_k, cat_v = refs
        else:
            acc, cat_k, cat_v = refs
    for half, dq_ref in zip(halves, dq_refs):
        dq_ref[0] = half[0]
    slab_blocks = acc.shape[0] // 2
    heads = dq_refs[0].shape[1]
    select = keys_ref.shape[1]
    rows = heads * BLOCK
    head_dim = kv.shape[3]
    scale = 1.0 / math.sqrt(head_dim)
    first = slab_ref[0] * slab_blocks
    me = me_ref[0]
    if call != FIRST:
        acc[...] = acc_in[...]
    else:
        kv[:slab_blocks] = prev_ref[...]
        kv[slab_blocks:] = own_ref[...]
        acc[...] = jnp.zeros_like(acc)
    key_pos = lax.broadcasted_iota(jnp.int32, (BLOCK, rows), 0)
    query_pos = lax.broadcasted_iota(jnp.int32, (BLOCK, rows), 1) % BLOCK
    causal = key_pos <= query_pos

    def query_block(slot, operand, row, out, out_row):
        b = me ^ slot
        q = qd_refs[operand][row, :heads].reshape(rows, head_dim)
        do = qd_refs[operand][row, heads:].reshape(rows, head_dim)
        entries = [keys_ref[first + b, j] for j in range(select)]
        places = [jnp.where(e < first, 0, slab_blocks) + ((e - first) & (slab_blocks - 1) ^ me) for e in entries]
        for j, place in enumerate(places):
            cat_k[pl.ds(j * BLOCK, BLOCK)] = kv[place, 0]
            cat_v[pl.ds(j * BLOCK, BLOCK)] = kv[place, 1]
        lanes = pl.ds(pl.multiple_of((first + b) * BLOCK, BLOCK), BLOCK)
        lse = jnp.concatenate([lse_ref[pl.ds(h, 1), lanes] for h in range(heads)], 1) * LOG2E
        delta = jnp.concatenate([delta_ref[pl.ds(h, 1), lanes] for h in range(heads)], 1)
        s = contract(cat_k[...], q, 1, 1)
        dp = contract(cat_v[...], do, 1, 1)
        p_parts = []
        for j in range(select):
            taken = lse if j == 0 else lse + jnp.where(entries[j] >= 0, 0.0, 1e30)
            p = jnp.exp2(s[j * BLOCK : (j + 1) * BLOCK] * (scale * LOG2E) - taken)
            p_parts.append(jnp.where(causal, p, 0.0) if j == 0 else p)
        p = jnp.concatenate(p_parts, 0)
        ds = (p * (dp - delta)).astype(jnp.bfloat16)
        dv = contract(p.astype(jnp.bfloat16), do, 1, 0)
        dk = contract(ds, q, 1, 0) * scale
        dq = contract(ds, cat_k[...], 0, 0) * scale
        dq_refs[out][out_row] = dq.astype(jnp.bfloat16).reshape(heads, BLOCK, head_dim)
        for j, place in enumerate(places):
            part = slice(j * BLOCK, (j + 1) * BLOCK)
            acc[place, 0] += dk[part]
            acc[place, 1] += dv[part]

    for block in blocks:
        query_block(*block)
    if call == LAST:
        at = 0
        for out in prev_out:
            out[...] = acc[at : at + out.shape[0]].astype(out.dtype)
            at += out.shape[0]
        own_out[...] = acc[slab_blocks:]


def block_grads(blocks, out_rows, slab, me, block_keys, lse, delta, pieces, halves, kept, call):
    slab_blocks = kept[0].shape[0] if call == FIRST else kept[0].shape[0] // 2
    head_dim = pieces[0].shape[3]
    heads = lse.shape[0]
    select = block_keys.shape[1]
    smem = pl.BlockSpec(memory_space=pltpu.SMEM)
    vmem = pl.BlockSpec(memory_space=pltpu.VMEM)
    wide = select * BLOCK
    macs = len(blocks) * heads * select * 5 * BLOCK * BLOCK * head_dim
    acc = jax.ShapeDtypeStruct((2 * slab_blocks, 2, BLOCK, head_dim), jnp.float32)
    out_shape = [jax.ShapeDtypeStruct((rows, heads, BLOCK, head_dim), jnp.bfloat16) for rows in out_rows]
    operands = [lse, delta, *pieces, *halves, *kept]
    if call == LAST:
        out_shape.append(jax.ShapeDtypeStruct((slab_blocks, 2, BLOCK, head_dim), jnp.float32))
        out_shape += [jax.ShapeDtypeStruct((count, 2, BLOCK, head_dim), jnp.bfloat16) for count in (2, slab_blocks - 4, 2)]
    elif call == FIRST:
        out_shape += [jax.ShapeDtypeStruct(acc.shape, jnp.bfloat16), acc]
    else:
        out_shape.append(acc)
    return pl.pallas_call(
        functools.partial(block_kernel, blocks, len(out_rows), len(halves), len(pieces), call),
        in_specs=[smem] * 3 + [vmem] * len(operands),
        out_specs=[vmem] * len(out_shape),
        out_shape=out_shape,
        scratch_shapes=[pltpu.VMEM(acc.shape, acc.dtype)] * (call == LAST) + [pltpu.VMEM((wide, head_dim), jnp.bfloat16)] * 2,
        compiler_params=pltpu.CompilerParams(vmem_limit_bytes=32 * 1024 * 1024 if slab_blocks > 8 else 16 * 1024 * 1024),
        cost_estimate=pl.CostEstimate(flops=2 * macs, bytes_accessed=8 * 1024 * 1024, transcendentals=0),
    )(slab, me, block_keys, *operands)


def pack_kernel(devices, fold_counts, kept, given, after_count, me_ref, *refs):
    count = len(fold_counts)
    sources, refs = refs[:count], refs[count + after_count :]
    pieces, gives, refs = refs[: len(kept)], refs[len(kept) : len(kept) + len(given)], refs[len(kept) + len(given) :]
    by_token, by_head, sems = refs[:count], refs[count : 2 * count], refs[-1]
    me = me_ref[0]
    targets = [(piece.at[0], 2 * m) for piece, m in zip(pieces, kept)]
    targets += [(give.at[i], 2 * m + 1) for give, group in zip(gives, given) for i, m in enumerate(group)]
    copies = [pltpu.make_async_copy(sources[i], by_token[i], sems.at[i]) for i in range(count)]
    for copy in copies:
        copy.start()
    at = 0
    for copy, source, target, fold_count in zip(copies, by_token, by_head, fold_counts):
        copy.wait()
        target[...] = jnp.swapaxes(source[...], 0, 1)
        heads = target.shape[0] * fold_count // devices
        for out, slot in targets:
            device = me ^ slot
            out[at : at + heads] = target[pl.ds(device // fold_count * heads, heads)]
        at += heads


def packed(me, arrays, fold_counts, uly_count, kept, rows, given, after):
    tokens, _, head_dim = arrays[0].shape
    tiles = sum(x.shape[1] * fold_count for x, fold_count in zip(arrays, fold_counts)) // uly_count
    vmem = pl.BlockSpec(memory_space=pltpu.VMEM)
    counts = [rows] * len(kept) + [len(group) for group in given]
    shapes = [jax.ShapeDtypeStruct((count, tiles, tokens, head_dim), arrays[0].dtype) for count in counts]
    return pl.pallas_call(
        functools.partial(pack_kernel, uly_count, fold_counts, kept, given, len(after)),
        in_specs=[pl.BlockSpec(memory_space=pltpu.SMEM)]
        + [pl.BlockSpec(memory_space=pltpu.HBM)] * len(arrays)
        + [pl.BlockSpec(memory_space=pl.ANY)] * len(after),
        out_specs=[vmem] * len(shapes),
        out_shape=shapes,
        scratch_shapes=[pltpu.VMEM(x.shape, x.dtype) for x in arrays]
        + [pltpu.VMEM((x.shape[1], tokens, head_dim), x.dtype) for x in arrays]
        + [pltpu.SemaphoreType.DMA((len(arrays),))],
        compiler_params=pltpu.CompilerParams(vmem_limit_bytes=8 * 1024 * 1024),
    )(me, *[pltpu.with_memory_space_constraint(x, pltpu.HBM) for x in arrays], *after)


def merge_kernel(count, *refs):
    got, outs = refs[count], refs[-count:]
    for i, out in enumerate(outs):
        out[1] = got[i]


def merged(pieces, got, after):
    count = len(pieces)
    vmem = pl.BlockSpec(memory_space=pltpu.VMEM)
    return pl.pallas_call(
        functools.partial(merge_kernel, count),
        in_specs=[vmem] * (count + 1 + len(after)),
        out_specs=[vmem] * count,
        out_shape=[jax.ShapeDtypeStruct(x.shape, x.dtype) for x in pieces],
        input_output_aliases={i: i for i in range(count)},
        compiler_params=pltpu.CompilerParams(vmem_limit_bytes=8 * 1024 * 1024),
    )(*map(held, pieces), got, *after)


def landed_kernel(*refs):
    pass


def landed(piece, after, flops):
    hold = pl.BlockSpec(memory_space=pl.ANY)
    return pl.pallas_call(
        landed_kernel,
        in_specs=[hold] * (1 + len(after)),
        out_specs=hold,
        out_shape=jax.ShapeDtypeStruct(piece.shape, piece.dtype),
        input_output_aliases={0: 0},
        cost_estimate=pl.CostEstimate(flops=flops, bytes_accessed=2**20, transcendentals=0),
    )(piece, *after)


def join_kernel(*refs):
    *pieces, out = refs
    for m, piece in enumerate(pieces):
        out[2 * m : 2 * m + 2] = piece[...]


def joined(pieces):
    vmem = pl.BlockSpec(memory_space=pltpu.VMEM)
    return pl.pallas_call(
        join_kernel,
        in_specs=[vmem] * len(pieces),
        out_specs=vmem,
        out_shape=jax.ShapeDtypeStruct((2 * len(pieces), *pieces[0].shape[1:]), pieces[0].dtype),
        compiler_params=pltpu.CompilerParams(vmem_limit_bytes=16 * 1024 * 1024),
        cost_estimate=pl.CostEstimate(flops=JOIN_COST, bytes_accessed=2**20, transcendentals=0),
    )(*pieces)


def add_kernel(first, after_count, own, back, *refs):
    for i, out in enumerate(refs[after_count:]):
        rows = slice(2 * (first + i), 2 * (first + i) + 2)
        out[...] = (own[rows] + back[2 * i : 2 * i + 2].astype(jnp.float32)).astype(out.dtype)


def added(first, own, back, after):
    vmem = pl.BlockSpec(memory_space=pltpu.VMEM)
    count = back.shape[0] // 2
    return pl.pallas_call(
        functools.partial(add_kernel, first, len(after)),
        in_specs=[vmem] * 2 + [vmem if x.ndim == 4 else pl.BlockSpec(memory_space=pltpu.HBM) for x in after],
        out_specs=[vmem] * count,
        out_shape=[jax.ShapeDtypeStruct((2, *back.shape[1:]), back.dtype)] * count,
        compiler_params=pltpu.CompilerParams(vmem_limit_bytes=8 * 1024 * 1024),
        cost_estimate=pl.CostEstimate(flops=ADD_COST, bytes_accessed=2**20, transcendentals=0),
    )(own, back, *[x if x.ndim == 4 else pltpu.with_memory_space_constraint(x, pltpu.HBM) for x in after])


def collect_kernel(chips, *refs):
    for m in range(chips):
        refs[-1][m] = refs[m][1]


def collected(chunks, after):
    vmem = pl.BlockSpec(memory_space=pltpu.VMEM)
    return pl.pallas_call(
        functools.partial(collect_kernel, len(chunks)),
        in_specs=[vmem] * len(chunks) + [pl.BlockSpec(memory_space=pl.ANY)] * len(after),
        out_specs=vmem,
        out_shape=jax.ShapeDtypeStruct((len(chunks), *chunks[0].shape[1:]), chunks[0].dtype),
        compiler_params=pltpu.CompilerParams(vmem_limit_bytes=8 * 1024 * 1024),
    )(*chunks, *after)


def unpack_kernel(chips, fold_count, me_ref, *refs):
    here, (got, *refs) = refs[:chips], refs[chips:]
    count = (len(refs) - 1) // 3
    outs, by_head, by_token, sems = refs[:count], refs[count : 2 * count], refs[2 * count : 3 * count], refs[-1]
    me = me_ref[0]
    for k in range(2 * chips):
        device = me ^ k
        part = here[k // 2][0] if k % 2 == 0 else got[k // 2]
        heads = part.shape[0] // count
        for i in range(count):
            by_head[i][pl.ds(device * heads, heads)] = part[i * heads : (i + 1) * heads]
    copies = [pltpu.make_async_copy(by_token[i], outs[i], sems.at[i]) for i in range(count)]
    for i in range(count):
        whole = by_head[i][...]
        if fold_count > 1:
            whole = whole.reshape(-1, fold_count, *whole.shape[1:]).astype(jnp.float32).sum(1).astype(whole.dtype)
        by_token[i][...] = jnp.swapaxes(whole, 0, 1)
        copies[i].start()
    for copy in copies:
        copy.wait()


def unpacked(me, here, got, count, fold_count):
    chips, tiles, tokens, head_dim = got.shape
    devices = 2 * chips
    vmem = pl.BlockSpec(memory_space=pltpu.VMEM)
    heads = devices * tiles // count
    shape = (tokens, heads // fold_count, head_dim)
    return pl.pallas_call(
        functools.partial(unpack_kernel, chips, fold_count),
        in_specs=[pl.BlockSpec(memory_space=pltpu.SMEM)] + [vmem] * (chips + 1),
        out_specs=[pl.BlockSpec(memory_space=pltpu.HBM)] * count,
        out_shape=[jax.ShapeDtypeStruct(shape, got.dtype)] * count,
        scratch_shapes=[pltpu.VMEM((heads, tokens, head_dim), got.dtype)] * count
        + [pltpu.VMEM(shape, got.dtype)] * count
        + [pltpu.SemaphoreType.DMA((count,))],
        compiler_params=pltpu.CompilerParams(vmem_limit_bytes=16 * 1024 * 1024),
    )(me, *here, got)


def passed_along(block, axis, distance):
    devices = range(lax.axis_size(axis))
    return lax.ppermute(block, axis, [(i - distance, i) for i in devices if i - distance in devices])


def swapped(block, k):
    if k == 0:
        return block
    return lax.ppermute(block, "uly", [(i, i ^ k) for i in range(lax.axis_size("uly"))])


def shards(queries, keys, values, grad_out, lse, delta, block_keys):
    uly_count = lax.axis_size("uly")
    head_total = queries.shape[1]
    fold_count = uly_count // keys.shape[1]
    heads = head_total // uly_count
    chips = uly_count // 2
    far = chips - 1
    me = lax.axis_index("uly").reshape(1)
    slab = lax.axis_index("blk").reshape(1)

    every, ends, mids = list(range(chips)), [0, far], list(range(1, far))
    *kv_pieces, give_kv = packed(me, [keys, values], [fold_count] * 2, uly_count, every, 2, [every], [])
    merged_kv = merged(kv_pieces, swapped(give_kv, 1), [])
    kv_pieces = [swapped(piece, 2 * m) for m, piece in enumerate(merged_kv)]
    own = joined(kv_pieces)
    pack = functools.partial(packed, me, [queries, grad_out], [1] * 2, uly_count)
    *qd_ends, give_ends, give_mids = pack(ends, 2, [ends, mids], merged_kv[:1])
    qd_here, qd_far = merged(qd_ends, swapped(give_ends, 1), [own])
    qd_far = landed(swapped(qd_far, 2 * far), [], SHORT)
    got_mids = swapped(give_mids, 1)
    firsts = [swapped(piece, 2 * m) for m, piece in zip(mids, pack(mids, 1, [], [own]))]
    seconds = [swapped(got_mids[i : i + 1], 2 * m) for i, m in enumerate(mids)]
    prev = passed_along(own, "blk", 1)

    grads = functools.partial(block_grads, slab=slab, me=me, block_keys=block_keys, lse=lse, delta=delta)
    blocks = [(2 * m + i, operand, i, operand, i) for operand, m in enumerate(ends) for i in range(2)]
    dq_here, dq_far, kv, acc = grads(blocks, [2, 2], pieces=[qd_here, qd_far], halves=[], kept=[own, prev], call=FIRST)
    blocks = [(2 * m, i, 0, i, 0) for i, m in enumerate(mids)]
    *halves, acc = grads(blocks, [1] * len(mids), pieces=firsts, halves=[], kept=[kv, acc], call=NEXT)
    blocks = [(2 * m + 1, i, 0, i, 1) for i, m in enumerate(mids)]
    outs = grads(blocks, [2] * len(mids), pieces=seconds, halves=halves, kept=[kv, acc], call=LAST)
    *dq_mid, own_grad, prev_here, prev_mid, prev_far = outs
    dq = [swapped(x, 2 * m) for m, x in enumerate([dq_here, *dq_mid, dq_far])]

    def back_added(part, first, after):
        total = added(first, own_grad, passed_along(part, "blk", -1), after)
        return [swapped(x, 2 * (first + i)) for i, x in enumerate(total)]

    kv_far = back_added(prev_far, far, [dq[far]])
    (grad_queries,) = unpacked(me, dq, swapped(collected(dq, []), 1), 1, 1)
    kv_mid = back_added(prev_mid, 1, dq[1:far] + kv_far)
    kv_here = back_added(prev_here, 0, kv_mid + [grad_queries])
    kv_grad = kv_here + kv_mid + kv_far
    got_kv = swapped(collected(kv_grad, []), 1)
    grad_keys, grad_values = unpacked(me, kv_grad, got_kv, 2, fold_count)
    return grad_queries, grad_keys, grad_values


def solution(mesh):
    spread = P(("blk", "uly"), None, None)
    return jax.shard_map(
        shards,
        mesh=mesh,
        in_specs=(spread, spread, spread, spread, P("uly", None), P("uly", None), P()),
        out_specs=(spread, spread, spread),
        check_vma=False,
    )
```

```python
import functools
import math

import jax
import jax.numpy as jnp
from jax import lax
from jax.experimental import pallas as pl
from jax.experimental.pallas import tpu as pltpu
from jax.sharding import PartitionSpec as P

BLOCK = 128
LOG2E = 1.4426950408889634
FIRST, NEXT, LAST = range(3)
SHORT, JOIN_COST, ADD_COST = 2 * 10**9, 10**10, 10**11


def contract(a, b, a_dim, b_dim):
    return lax.dot_general(a, b, (((a_dim,), (b_dim,)), ((), ())), preferred_element_type=jnp.float32)


def held(x):
    return pltpu.with_memory_space_constraint(x, pltpu.VMEM)


def block_kernel(blocks, out_count, half_count, operand_count, call, slab_ref, me_ref, keys_ref, lse_ref, delta_ref, *refs):
    qd_refs, refs = refs[:operand_count], refs[operand_count:]
    halves, refs = refs[:half_count], refs[half_count:]
    if call == FIRST:
        (own_ref, prev_ref), dq_refs, (kv, acc, cat_k, cat_v) = refs[:2], refs[2 : 2 + out_count], refs[2 + out_count :]
    else:
        (kv, acc_in), dq_refs, refs = refs[:2], refs[2 : 2 + out_count], refs[2 + out_count :]
        if call == LAST:
            own_out, *prev_out, acc, cat_k, cat_v = refs
        else:
            acc, cat_k, cat_v = refs
    for half, dq_ref in zip(halves, dq_refs if call == LAST else dq_refs[-half_count:]):
        dq_ref[: half.shape[0]] = half[...]
    slab_blocks = acc.shape[0] // 2
    heads = dq_refs[0].shape[1]
    select = keys_ref.shape[1]
    rows = heads * BLOCK
    head_dim = kv.shape[3]
    scale = 1.0 / math.sqrt(head_dim)
    first = slab_ref[0] * slab_blocks
    me = me_ref[0]
    if call != FIRST:
        acc[...] = acc_in[...]
    else:
        kv[:slab_blocks] = prev_ref[...]
        kv[slab_blocks:] = own_ref[...]
        acc[...] = jnp.zeros_like(acc)
    key_pos = lax.broadcasted_iota(jnp.int32, (BLOCK, rows), 0)
    query_pos = lax.broadcasted_iota(jnp.int32, (BLOCK, rows), 1) % BLOCK
    causal = key_pos <= query_pos

    def query_block(slot, operand, row, out, out_row):
        b = me ^ slot
        q = qd_refs[operand][row, :heads].reshape(rows, head_dim)
        do = qd_refs[operand][row, heads:].reshape(rows, head_dim)
        entries = [keys_ref[first + b, j] for j in range(select)]
        places = [jnp.where(e < first, 0, slab_blocks) + ((e - first) & (slab_blocks - 1) ^ me) for e in entries]
        for j, place in enumerate(places):
            cat_k[pl.ds(j * BLOCK, BLOCK)] = kv[place, 0]
            cat_v[pl.ds(j * BLOCK, BLOCK)] = kv[place, 1]
        lanes = pl.ds(pl.multiple_of((first + b) * BLOCK, BLOCK), BLOCK)
        lse = jnp.concatenate([lse_ref[pl.ds(h, 1), lanes] for h in range(heads)], 1) * LOG2E
        delta = jnp.concatenate([delta_ref[pl.ds(h, 1), lanes] for h in range(heads)], 1)
        s = contract(cat_k[...], q, 1, 1)
        dp = contract(cat_v[...], do, 1, 1)
        p_parts = []
        for j in range(select):
            taken = lse if j == 0 else lse + jnp.where(entries[j] >= 0, 0.0, 1e30)
            p = jnp.exp2(s[j * BLOCK : (j + 1) * BLOCK] * (scale * LOG2E) - taken)
            p_parts.append(jnp.where(causal, p, 0.0) if j == 0 else p)
        p = jnp.concatenate(p_parts, 0)
        ds = (p * (dp - delta)).astype(jnp.bfloat16)
        dv = contract(p.astype(jnp.bfloat16), do, 1, 0)
        dk = contract(ds, q, 1, 0) * scale
        dq = contract(ds, cat_k[...], 0, 0) * scale
        dq_refs[out][out_row] = dq.astype(jnp.bfloat16).reshape(heads, BLOCK, head_dim)
        for j, place in enumerate(places):
            part = slice(j * BLOCK, (j + 1) * BLOCK)
            acc[place, 0] += dk[part]
            acc[place, 1] += dv[part]

    for block in blocks:
        query_block(*block)
    if call == LAST:
        at = 0
        for out in prev_out:
            out[...] = acc[at : at + out.shape[0]].astype(out.dtype)
            at += out.shape[0]
        own_out[...] = acc[slab_blocks:]


def block_grads(blocks, out_rows, slab, me, block_keys, lse, delta, pieces, halves, kept, call):
    slab_blocks = kept[0].shape[0] if call == FIRST else kept[0].shape[0] // 2
    head_dim = pieces[0].shape[3]
    heads = lse.shape[0]
    select = block_keys.shape[1]
    smem = pl.BlockSpec(memory_space=pltpu.SMEM)
    vmem = pl.BlockSpec(memory_space=pltpu.VMEM)
    wide = select * BLOCK
    macs = len(blocks) * heads * select * 5 * BLOCK * BLOCK * head_dim
    acc = jax.ShapeDtypeStruct((2 * slab_blocks, 2, BLOCK, head_dim), jnp.float32)
    out_shape = [jax.ShapeDtypeStruct((rows, heads, BLOCK, head_dim), jnp.bfloat16) for rows in out_rows]
    operands = [lse, delta, *pieces, *halves, *kept]
    if call == LAST:
        out_shape.append(jax.ShapeDtypeStruct((slab_blocks, 2, BLOCK, head_dim), jnp.float32))
        out_shape += [jax.ShapeDtypeStruct((count, 2, BLOCK, head_dim), jnp.bfloat16) for count in (2, slab_blocks - 4, 2)]
    elif call == FIRST:
        out_shape += [jax.ShapeDtypeStruct(acc.shape, jnp.bfloat16), acc]
    else:
        out_shape.append(acc)
    return pl.pallas_call(
        functools.partial(block_kernel, blocks, len(out_rows), len(halves), len(pieces), call),
        in_specs=[smem] * 3 + [vmem] * len(operands),
        out_specs=[vmem] * len(out_shape),
        out_shape=out_shape,
        scratch_shapes=[pltpu.VMEM(acc.shape, acc.dtype)] * (call == LAST) + [pltpu.VMEM((wide, head_dim), jnp.bfloat16)] * 2,
        compiler_params=pltpu.CompilerParams(vmem_limit_bytes=32 * 1024 * 1024 if slab_blocks > 8 else 16 * 1024 * 1024),
        cost_estimate=pl.CostEstimate(flops=2 * macs, bytes_accessed=8 * 1024 * 1024, transcendentals=0),
    )(slab, me, block_keys, *operands)


def pack_kernel(devices, fold_counts, kept, given, after_count, me_ref, *refs):
    count = len(fold_counts)
    sources, refs = refs[:count], refs[count + after_count :]
    pieces, gives, refs = refs[: len(kept)], refs[len(kept) : len(kept) + len(given)], refs[len(kept) + len(given) :]
    by_token, by_head, sems = refs[:count], refs[count : 2 * count], refs[-1]
    me = me_ref[0]
    targets = [(piece.at[0], 2 * m) for piece, m in zip(pieces, kept)]
    targets += [(give.at[i], 2 * m + 1) for give, group in zip(gives, given) for i, m in enumerate(group)]
    copies = [pltpu.make_async_copy(sources[i], by_token[i], sems.at[i]) for i in range(count)]
    for copy in copies:
        copy.start()
    at = 0
    for copy, source, target, fold_count in zip(copies, by_token, by_head, fold_counts):
        copy.wait()
        target[...] = jnp.swapaxes(source[...], 0, 1)
        heads = target.shape[0] * fold_count // devices
        for out, slot in targets:
            device = me ^ slot
            out[at : at + heads] = target[pl.ds(device // fold_count * heads, heads)]
        at += heads


def packed(me, arrays, fold_counts, uly_count, kept, rows, given, after):
    tokens, _, head_dim = arrays[0].shape
    tiles = sum(x.shape[1] * fold_count for x, fold_count in zip(arrays, fold_counts)) // uly_count
    vmem = pl.BlockSpec(memory_space=pltpu.VMEM)
    counts = [rows] * len(kept) + [len(group) for group in given]
    shapes = [jax.ShapeDtypeStruct((count, tiles, tokens, head_dim), arrays[0].dtype) for count in counts]
    return pl.pallas_call(
        functools.partial(pack_kernel, uly_count, fold_counts, kept, given, len(after)),
        in_specs=[pl.BlockSpec(memory_space=pltpu.SMEM)]
        + [pl.BlockSpec(memory_space=pltpu.HBM)] * len(arrays)
        + [pl.BlockSpec(memory_space=pl.ANY)] * len(after),
        out_specs=[vmem] * len(shapes),
        out_shape=shapes,
        scratch_shapes=[pltpu.VMEM(x.shape, x.dtype) for x in arrays]
        + [pltpu.VMEM((x.shape[1], tokens, head_dim), x.dtype) for x in arrays]
        + [pltpu.SemaphoreType.DMA((len(arrays),))],
        compiler_params=pltpu.CompilerParams(vmem_limit_bytes=8 * 1024 * 1024),
    )(me, *[pltpu.with_memory_space_constraint(x, pltpu.HBM) for x in arrays], *after)


def merge_kernel(count, *refs):
    pieces, got, outs = refs[:count], refs[count], refs[-count:]
    for i, out in enumerate(outs):
        out[0] = pieces[i][0]
        out[1] = got[i]


def merged(pieces, got, after):
    count = len(pieces)
    vmem = pl.BlockSpec(memory_space=pltpu.VMEM)
    return pl.pallas_call(
        functools.partial(merge_kernel, count),
        in_specs=[vmem] * (count + 1 + len(after)),
        out_specs=[vmem] * count,
        out_shape=[jax.ShapeDtypeStruct(x.shape, x.dtype) for x in pieces],
        input_output_aliases={i: i for i in range(count)},
        compiler_params=pltpu.CompilerParams(vmem_limit_bytes=8 * 1024 * 1024),
    )(*map(held, pieces), got, *after)


def landed_kernel(*refs):
    pass


def landed(piece, after, flops):
    hold = pl.BlockSpec(memory_space=pl.ANY)
    return pl.pallas_call(
        landed_kernel,
        in_specs=[hold] * (1 + len(after)),
        out_specs=hold,
        out_shape=jax.ShapeDtypeStruct(piece.shape, piece.dtype),
        input_output_aliases={0: 0},
        cost_estimate=pl.CostEstimate(flops=flops, bytes_accessed=2**20, transcendentals=0),
    )(piece, *after)


def join_kernel(*refs):
    *pieces, out = refs
    for m, piece in enumerate(pieces):
        out[2 * m : 2 * m + 2] = piece[...]


def joined(pieces):
    vmem = pl.BlockSpec(memory_space=pltpu.VMEM)
    return pl.pallas_call(
        join_kernel,
        in_specs=[vmem] * len(pieces),
        out_specs=vmem,
        out_shape=jax.ShapeDtypeStruct((2 * len(pieces), *pieces[0].shape[1:]), pieces[0].dtype),
        compiler_params=pltpu.CompilerParams(vmem_limit_bytes=16 * 1024 * 1024),
        cost_estimate=pl.CostEstimate(flops=JOIN_COST, bytes_accessed=2**20, transcendentals=0),
    )(*pieces)


def add_kernel(first, after_count, own, back, *refs):
    for i, out in enumerate(refs[after_count:]):
        rows = slice(2 * (first + i), 2 * (first + i) + 2)
        out[...] = (own[rows] + back[2 * i : 2 * i + 2].astype(jnp.float32)).astype(out.dtype)


def added(first, own, back, after):
    vmem = pl.BlockSpec(memory_space=pltpu.VMEM)
    count = back.shape[0] // 2
    return pl.pallas_call(
        functools.partial(add_kernel, first, len(after)),
        in_specs=[vmem] * 2 + [vmem if x.ndim == 4 else pl.BlockSpec(memory_space=pltpu.HBM) for x in after],
        out_specs=[vmem] * count,
        out_shape=[jax.ShapeDtypeStruct((2, *back.shape[1:]), back.dtype)] * count,
        compiler_params=pltpu.CompilerParams(vmem_limit_bytes=8 * 1024 * 1024),
        cost_estimate=pl.CostEstimate(flops=ADD_COST, bytes_accessed=2**20, transcendentals=0),
    )(own, back, *[x if x.ndim == 4 else pltpu.with_memory_space_constraint(x, pltpu.HBM) for x in after])


def collect_kernel(chips, *refs):
    for m in range(chips):
        refs[-1][m] = refs[m][1]


def collected(chunks, after):
    vmem = pl.BlockSpec(memory_space=pltpu.VMEM)
    return pl.pallas_call(
        functools.partial(collect_kernel, len(chunks)),
        in_specs=[vmem] * len(chunks) + [pl.BlockSpec(memory_space=pl.ANY)] * len(after),
        out_specs=vmem,
        out_shape=jax.ShapeDtypeStruct((len(chunks), *chunks[0].shape[1:]), chunks[0].dtype),
        compiler_params=pltpu.CompilerParams(vmem_limit_bytes=8 * 1024 * 1024),
    )(*chunks, *after)


def unpack_kernel(chips, fold_count, me_ref, *refs):
    here, (got, *refs) = refs[:chips], refs[chips:]
    count = (len(refs) - 1) // 3
    outs, by_head, by_token, sems = refs[:count], refs[count : 2 * count], refs[2 * count : 3 * count], refs[-1]
    me = me_ref[0]
    for k in range(2 * chips):
        device = me ^ k
        part = here[k // 2][0] if k % 2 == 0 else got[k // 2]
        heads = part.shape[0] // count
        for i in range(count):
            by_head[i][pl.ds(device * heads, heads)] = part[i * heads : (i + 1) * heads]
    copies = [pltpu.make_async_copy(by_token[i], outs[i], sems.at[i]) for i in range(count)]
    for i in range(count):
        whole = by_head[i][...]
        if fold_count > 1:
            whole = whole.reshape(-1, fold_count, *whole.shape[1:]).astype(jnp.float32).sum(1).astype(whole.dtype)
        by_token[i][...] = jnp.swapaxes(whole, 0, 1)
        copies[i].start()
    for copy in copies:
        copy.wait()


def unpacked(me, here, got, count, fold_count):
    chips, tiles, tokens, head_dim = got.shape
    devices = 2 * chips
    vmem = pl.BlockSpec(memory_space=pltpu.VMEM)
    heads = devices * tiles // count
    shape = (tokens, heads // fold_count, head_dim)
    return pl.pallas_call(
        functools.partial(unpack_kernel, chips, fold_count),
        in_specs=[pl.BlockSpec(memory_space=pltpu.SMEM)] + [vmem] * (chips + 1),
        out_specs=[pl.BlockSpec(memory_space=pltpu.HBM)] * count,
        out_shape=[jax.ShapeDtypeStruct(shape, got.dtype)] * count,
        scratch_shapes=[pltpu.VMEM((heads, tokens, head_dim), got.dtype)] * count
        + [pltpu.VMEM(shape, got.dtype)] * count
        + [pltpu.SemaphoreType.DMA((count,))],
        compiler_params=pltpu.CompilerParams(vmem_limit_bytes=16 * 1024 * 1024),
    )(me, *here, got)


def passed_along(block, axis, distance):
    devices = range(lax.axis_size(axis))
    return lax.ppermute(block, axis, [(i - distance, i) for i in devices if i - distance in devices])


def swapped(block, k):
    if k == 0:
        return block
    return lax.ppermute(block, "uly", [(i, i ^ k) for i in range(lax.axis_size("uly"))])


def shards(queries, keys, values, grad_out, lse, delta, block_keys):
    uly_count = lax.axis_size("uly")
    head_total = queries.shape[1]
    fold_count = uly_count // keys.shape[1]
    heads = head_total // uly_count
    chips = uly_count // 2
    far = chips - 1
    me = lax.axis_index("uly").reshape(1)
    slab = lax.axis_index("blk").reshape(1)

    every, ends, mids = list(range(chips)), [0, far], list(range(1, far))
    *kv_pieces, give_kv = packed(me, [keys, values], [fold_count] * 2, uly_count, every, 2, [every], [])
    merged_kv = merged(kv_pieces, swapped(give_kv, 1), [])
    kv_pieces = [swapped(piece, 2 * m) for m, piece in enumerate(merged_kv)]
    own = joined(kv_pieces)
    pack = functools.partial(packed, me, [queries, grad_out], [1] * 2, uly_count)
    *qd_ends, give_ends, give_mids = pack(ends, 2, [ends, mids], merged_kv[:1])
    qd_here, qd_far = merged(qd_ends, swapped(give_ends, 1), [own])
    qd_far = landed(swapped(qd_far, 2 * far), [], SHORT)
    got_mids = swapped(give_mids, 1)
    firsts = [swapped(piece, 2 * m) for m, piece in zip(mids, pack(mids, 1, [], [own]))]
    seconds = [swapped(got_mids[i : i + 1], 2 * m) for i, m in enumerate(mids)]
    prev = passed_along(own, "blk", 1)

    grads = functools.partial(block_grads, slab=slab, me=me, block_keys=block_keys, lse=lse, delta=delta)
    blocks = [(2 * m + i, operand, i, operand, i) for operand, m in enumerate(ends) for i in range(2)]
    dq_here, dq_far, kv, acc = grads(blocks, [2, 2], pieces=[qd_here, qd_far], halves=[], kept=[own, prev], call=FIRST)
    blocks = [(2 * m, i, 0, i, 0) for i, m in enumerate(mids)]
    *halves, dq_far, acc = grads(blocks, [1] * len(mids) + [2], pieces=firsts, halves=[dq_far], kept=[kv, acc], call=NEXT)
    blocks = [(2 * m + 1, i, 0, i, 1) for i, m in enumerate(mids)]
    outs = grads(blocks, [2] * len(mids), pieces=seconds, halves=halves, kept=[kv, acc], call=LAST)
    *dq_mid, own_grad, prev_here, prev_mid, prev_far = outs
    dq = [swapped(x, 2 * m) for m, x in enumerate([dq_here, *dq_mid, dq_far])]

    def back_added(part, first, after):
        total = added(first, own_grad, passed_along(part, "blk", -1), after)
        return [swapped(x, 2 * (first + i)) for i, x in enumerate(total)]

    kv_far = back_added(prev_far, far, [dq[far]])
    (grad_queries,) = unpacked(me, dq, swapped(collected(dq, []), 1), 1, 1)
    kv_mid = back_added(prev_mid, 1, dq[1:far] + kv_far)
    kv_here = back_added(prev_here, 0, kv_mid + [grad_queries])
    kv_grad = kv_here + kv_mid + kv_far
    got_kv = swapped(collected(kv_grad, []), 1)
    grad_keys, grad_values = unpacked(me, kv_grad, got_kv, 2, fold_count)
    return grad_queries, grad_keys, grad_values


def solution(mesh):
    spread = P(("blk", "uly"), None, None)
    return jax.shard_map(
        shards,
        mesh=mesh,
        in_specs=(spread, spread, spread, spread, P("uly", None), P("uly", None), P()),
        out_specs=(spread, spread, spread),
        check_vma=False,
    )
```
